32 devices in a mesh: band: 8 (over y, x, core), tile: 4 (over z).
Axes of the slice: x: 2, y: 2, z: 4, core: 2. Of those that a mesh axis runs over, the one named last changes fastest.
Arguments:
- coarse_source: float32 [128, 512], P('band', 'tile'), may hold values from 0.1 to 10
- coarse_target: float32 [128, 512], P('band', 'tile'), may hold values from 0.1 to 10
- target_offset: float32 [1024, 128], P(('band', 'tile')), may hold values from -4 to 122, as said below
- source_mass: float32 [1024, 128], P(('band', 'tile')), may hold values from 0.003 to 10
- target_mass: float32 [1024, 128], P(('band', 'tile')), may hold values from 0.1 to 10
- cell_count: int32 [1024], P(('band', 'tile')), may hold values from 1 to 128
- pair_source: int32 [16384], P(('band', 'tile')), may hold values from 0 to 32, as said below
- pair_target: int32 [16384], P(('band', 'tile')), may hold values from 0 to 1023, as said below
Outputs:
- scaling_u: float32 [128, 512], P('band', 'tile')
- scaling_v: float32 [128, 512], P('band', 'tile')
- source_potential: float32 [1024, 128], P(('band', 'tile'))
- target_potential: float32 [1024, 128], P(('band', 'tile'))
The draws below stay inside these ranges and needn't reach their ends.
Inputs may be any that keep to these rules, and one draw needn't show every extreme that they name: `target_offset`: A float of order one in each cell; in some tiles it may carry a large common level. `pair_source`: on each device, slot l < 32 is live with local source tile l; every local source tile appears; the live slots come first on each device, the others hold 32; on some device all 512 slots are live. `pair_target`: A live slot of slot index l < 32 on device d targets tile d * 32 + l; any live slot targets a tile of its device's band or an adjacent band, in any longitude block; an unused slot holds its device's first tile.
All inputs are finite; a program needn't handle non-finite values.
Results may differ from the reference program's by a relative error of at most 0.000075.
Values sent between devices are 32-bit elements; how exact they have to be, the bound alone decides.
A program may use at most 64 MiB of HBM per device.

```python
import math
import jax
import jax.numpy as jnp
from jax import lax

TILE = 128
CR = 16
STD = 32
PD = 512
COARSE_ITERS = 2
NR = 128
NC = 512
TILES = 1024
PAIRS = 16384
N_BAND = 8
N_TILE = 4


def build_pairs(key):
    key = jax.random.fold_in(key, 17)
    keys = jax.random.split(key, 6)
    count = N_BAND * N_TILE
    device = jnp.arange(count, dtype=jnp.int32)[:, None]
    slot = jnp.arange(PD, dtype=jnp.int32)[None, :]
    spread = jax.random.randint(keys[0], (count,), 0, 1000)
    hottest = jax.random.randint(keys[1], (), 0, count)
    extra = (PD - STD) * spread // 999
    extra = jnp.where(jnp.arange(count, dtype=jnp.int32) == hottest, PD - STD, extra)
    live = STD + extra[:, None]
    random_source = jax.random.randint(keys[2], (count, PD), 0, STD)
    source = jnp.where(slot < STD, jnp.minimum(slot, STD - 1), jnp.where(slot < live, random_source, STD))
    band_step = jax.random.randint(keys[3], (count, PD), -1, 2)
    column = jax.random.randint(keys[4], (count, PD), 0, N_TILE)
    local_step = jax.random.randint(keys[5], (count, PD), -3, 4)
    band = jnp.clip(device // N_TILE + band_step, 0, N_BAND - 1)
    local = jnp.clip(random_source + local_step, 0, STD - 1)
    far_target = (band * N_TILE + column) * STD + local
    own_target = device * STD + jnp.minimum(slot, STD - 1)
    target = jnp.where(slot < STD, own_target, jnp.where(slot < live, far_target, device * STD))
    return (source.reshape(-1).astype(jnp.int32), target.reshape(-1).astype(jnp.int32))


def draw_pair_source(key, part):
    return build_pairs(key)[0]


def draw_pair_target(key, part):
    return build_pairs(key)[1]


def draw_target_offset(key, part):
    keys = jax.random.split(jax.random.fold_in(key, 5), 4)
    side = jax.random.randint(keys[2], (TILES, 1), 0, 2)
    edge_col = jnp.where(side == 0, 0, TILE - 1)
    at_edge = jnp.arange(TILE, dtype=jnp.int32)[None, :] == edge_col
    level = jax.random.randint(keys[1], (TILES, 1), 0, 4).astype(jnp.float32) * 3.0
    rough = jnp.clip(-2.5 + 0.5 * jax.random.normal(keys[0], (TILES, TILE), jnp.float32), -4.0, -1.0)
    bump = jnp.clip(1.0 + 0.5 * jax.random.normal(keys[3], (TILES, 1), jnp.float32), 0.0, 2.0)
    return level + jnp.where(at_edge, bump, rough)


def draw_source_mass(key, part):
    keys = jax.random.split(jax.random.fold_in(key, 23), 3)
    spot = jax.random.randint(keys[2], (TILES, 1), 0, 8)
    at_spot = jnp.arange(TILE, dtype=jnp.int32)[None, :] == spot
    rest = jnp.exp(jax.random.uniform(keys[0], (TILES, TILE), jnp.float32, math.log(0.003), math.log(0.03)))
    high = jnp.exp(jax.random.uniform(keys[1], (TILES, 1), jnp.float32, math.log(3.0), math.log(10.0)))
    return jnp.clip(jnp.where(at_spot, high, rest), 0.003, 10.0)


def plant(values, key, smallest, high):
    index_at = [jax.random.randint(jax.random.fold_in(key, axis), (), 0, length) for axis, length in enumerate(values.shape)]
    widest = values.shape.index(max(values.shape))
    next_to = index_at[:widest] + [(index_at[widest] + 1) % values.shape[widest]] + index_at[widest + 1:]
    return values.at[tuple(index_at)].set(smallest).at[tuple(next_to)].set(high)


def steps_of(rng, dims, cuts, low, high):
    level = 1.0
    for axis_at, parts in cuts:
        steps = jax.random.uniform(jax.random.fold_in(jax.random.fold_in(rng, 6), axis_at), (parts,), jnp.float32, low / len(cuts), high / len(cuts))
        level = level * jnp.repeat(jnp.exp(steps), dims[axis_at] // parts).reshape((-1,) + (1,) * (len(dims) - 1 - axis_at))
    return level


def setup_inputs(seed: int = 0) -> dict:
    splits = jax.random.split(jax.random.key(seed), 9)
    coarse_source = jnp.clip(jnp.exp(math.log(10.0) - 4.6051702 * jax.random.uniform(splits[0], (NR, NC), jnp.float32) ** steps_of(splits[0], (NR, NC), ((0, 8), (1, 4)), -0.2, 0.2)), 0.1, 10.0)
    coarse_target = jnp.clip(jnp.exp(math.log(10.0) - 4.6051702 * jax.random.uniform(splits[1], (NR, NC), jnp.float32) ** steps_of(splits[1], (NR, NC), ((0, 8), (1, 4)), -0.2, 0.2)), 0.1, 10.0)
    target_offset = draw_target_offset(jax.random.fold_in(splits[8], 71), 0)
    source_mass = draw_source_mass(jax.random.fold_in(splits[8], 71), 0)
    target_mass = jnp.clip(jnp.exp(math.log(10.0) - 4.6051702 * jax.random.uniform(splits[4], (TILES, TILE), jnp.float32) ** steps_of(splits[4], (TILES, TILE), ((0, 32),), -0.2, 0.2)), 0.1, 10.0)
    cell_count = plant(jax.random.randint(splits[5], (TILES,), 1, 129), jax.random.fold_in(splits[5], 1), 1, 128).astype(jnp.int32)
    pair_source = draw_pair_source(jax.random.fold_in(splits[8], 71), 0)
    pair_target = draw_pair_target(jax.random.fold_in(splits[8], 71), 0)
    return dict(coarse_source=coarse_source, coarse_target=coarse_target, target_offset=target_offset, source_mass=source_mass, target_mass=target_mass, cell_count=cell_count, pair_source=pair_source, pair_target=pair_target)


entropy = 0.5
damping = 0.8
coarse_power = 0.8
kernel_taps = [math.exp(-0.125 * offset * offset) for offset in range(-4, 5)]


def blur(padded, rows, cols):
    across = kernel_taps[0] * padded[0:rows, :]
    for offset in range(1, 9):
        across = across + kernel_taps[offset] * padded[offset:offset + rows, :]
    result = kernel_taps[0] * across[:, 0:cols]
    for offset in range(1, 9):
        result = result + kernel_taps[offset] * across[:, offset:offset + cols]
    return result


def place(tile_index):
    device = tile_index // STD
    row = (device // N_TILE) * STD + tile_index % STD
    col = (device % N_TILE) * TILE
    return row.astype(jnp.float32), col.astype(jnp.float32)


def pair_cost(drow, dcol):
    cost_unit = float(NC * NC) / 4.0
    cell = jnp.arange(TILE, dtype=jnp.int32).astype(jnp.float32)
    diff = dcol[:, None, None] + cell[None, :, None] - cell[None, None, :]
    return (drow[:, None, None] * drow[:, None, None] + diff * diff) / cost_unit


def row_block(inputs):
    drow, dcol, fields = inputs
    score = fields[:, None, :] - pair_cost(drow, dcol) / entropy
    top = jnp.max(score, axis=2)
    total = jnp.sum(jnp.exp(score - top[:, :, None]), axis=2)
    return top, total


def col_block(inputs):
    drow, dcol, fields = inputs
    score = fields[:, :, None] - pair_cost(drow, dcol) / entropy
    top = jnp.max(score, axis=1)
    total = jnp.sum(jnp.exp(score - top[:, None, :]), axis=1)
    return top, total


def reference(coarse_source, coarse_target, target_offset, source_mass, target_mass, cell_count, pair_source, pair_target):
    rows, cols = coarse_source.shape
    scaling_v = jnp.ones_like(coarse_target)
    scaling_u = scaling_v
    for step in range(COARSE_ITERS):
        scaling_u = (coarse_source / blur(jnp.pad(scaling_v, 4), rows, cols)) ** coarse_power
        scaling_v = (coarse_target / blur(jnp.pad(scaling_u, 4), rows, cols)) ** coarse_power
    parent = jnp.log(scaling_v).reshape(N_BAND, CR, N_TILE, TILE).transpose(0, 2, 1, 3)
    parent = jnp.repeat(parent, STD // CR, axis=2).reshape(TILES, TILE)
    target_field = (target_offset + entropy * parent) / entropy + jnp.log(target_mass)
    slot = jnp.arange(PAIRS, dtype=jnp.int32)
    valid = pair_source < STD
    src_global = ((slot // PD) * STD + jnp.minimum(pair_source, STD - 1)).astype(jnp.int32)
    src_row, src_col = place(src_global)
    tgt_row, tgt_col = place(pair_target)
    drow = (src_row - tgt_row).reshape(-1, 256)
    dcol = (src_col - tgt_col).reshape(-1, 256)
    tops, totals = lax.map(row_block, (drow, dcol, target_field[pair_target].reshape(-1, 256, TILE)))
    tops = tops.reshape(PAIRS, TILE)
    totals = totals.reshape(PAIRS, TILE)
    neg = jnp.float32(-jnp.inf)
    peak = jnp.full((TILES, TILE), neg, jnp.float32).at[src_global].max(jnp.where(valid[:, None], tops, neg))
    weighted = jnp.where(valid[:, None], totals * jnp.exp(tops - peak[src_global]), jnp.float32(0.0))
    summed = jnp.zeros((TILES, TILE), jnp.float32).at[src_global].add(weighted)
    source_potential = -damping * entropy * (peak + jnp.log(summed))
    active = jnp.arange(TILE, dtype=jnp.int32)[None, :] < cell_count[:, None]
    source_field = jnp.where(active, source_potential / entropy + jnp.log(source_mass), neg)
    tops, totals = lax.map(col_block, (drow, dcol, source_field[src_global].reshape(-1, 256, TILE)))
    tops = tops.reshape(PAIRS, TILE)
    totals = totals.reshape(PAIRS, TILE)
    peak = jnp.full((TILES, TILE), neg, jnp.float32).at[pair_target].max(jnp.where(valid[:, None], tops, neg))
    weighted = jnp.where(valid[:, None], totals * jnp.exp(tops - peak[pair_target]), jnp.float32(0.0))
    summed = jnp.zeros((TILES, TILE), jnp.float32).at[pair_target].add(weighted)
    target_potential = -damping * entropy * (peak + jnp.log(summed))
    return scaling_u, scaling_v, source_potential, target_potential
```

```python
import functools
import math

import jax
import jax.numpy as jnp
from jax import lax
from jax.experimental import pallas as pl
from jax.experimental.pallas import tpu as pltpu
from jax.sharding import PartitionSpec as P

COARSE_ITERS = 2
REACH = 4
entropy = 0.5
damping = 0.8
coarse_power = 0.8
taps = [math.exp(-0.125 * k * k) for k in range(-REACH, REACH + 1)]
MESH = pl.DeviceIdType.MESH
NT = (((1,), (1,)), ((), ()))
NN = (((1,), (0,)), ((), ()))


def halves(x):
    high = x.astype(jnp.bfloat16)
    low = (x - high.astype(jnp.float32)).astype(jnp.bfloat16)
    return high, low


def dot(a, b):
    a_high, a_low = halves(a)
    b_high, b_low = halves(b)
    one = functools.partial(
        lax.dot_general, dimension_numbers=NN, preferred_element_type=jnp.float32
    )
    return one(a_high, b_high) + (one(a_high, b_low) + one(a_low, b_high))


def column_to_row(col, tiles):
    out = []
    for at in range(0, tiles, 128):
        eye = lax.broadcasted_iota(jnp.int32, (128, 128), 0) == lax.broadcasted_iota(
            jnp.int32, (128, 128), 1
        )
        part = jnp.where(eye, col[at : at + 128], 0.0)
        out.append(jnp.sum(part, axis=0, keepdims=True))
    return jnp.concatenate(out, axis=1)


def kernel(
    n_band,
    n_tile,
    cs_ref,
    ct_ref,
    off_ref,
    sm_ref,
    tm_ref,
    cnt_ref,
    pair_ref,
    u_ref,
    v_ref,
    sp_ref,
    tp_ref,
    coarse,
    ext,
    pairs,
    win1,
    win2,
    count1,
    count2,
    mix,
    c_send,
    c_recv,
    p_send,
    p_recv,
    w1_send,
    w1_recv,
    w2_send,
    w2_recv,
):
    rows, cols = cs_ref.shape
    tiles, width = off_ref.shape
    prow = pair_ref.shape[0] // 2
    band = lax.axis_index("band")
    tile = lax.axis_index("tile")
    f32 = jnp.float32
    keep = rows

    barrier = pltpu.get_barrier_semaphore()
    has_band = {-1: band > 0, 0: True, 1: band < n_band - 1}

    def when(cond, body):
        if cond is True:
            body()
        else:
            pl.when(cond)(body)

    partners = [
        (db, k) for db in (-1, 0, 1) for k in range(n_tile) if (db, k) != (0, 0)
    ]

    def device(db, k):
        return (band + db, lax.rem(tile + k, n_tile))

    for db, k in partners:

        def greet(db=db, k=k):
            pl.semaphore_signal(barrier, inc=1, device_id=device(db, k), device_id_type=MESH)

        when(has_band[db], greet)

    coarse[1, 1, 0:rows] = cs_ref[...]
    coarse[1, 1, rows : 2 * rows] = ct_ref[...]
    pairs[1, tile] = pair_ref[...]
    for db in (-1, 1):

        def blank(db=db):
            for dt in (-1, 0, 1):
                coarse[1 + db, 1 + dt] = jnp.zeros((2 * rows, cols), f32)
            for t in range(n_tile):
                pairs[1 + db, t] = jnp.full(pair_ref.shape, -1, jnp.int32)
                win1[1 + db, t] = jnp.zeros((tiles, width), f32)
                win2[1 + db, t] = jnp.zeros((tiles, width), f32)

        pl.when(jnp.logical_not(has_band[db]))(blank)
    for dt in (-1, 1):
        here = tile + dt

        @pl.when(jnp.logical_or(here < 0, here > n_tile - 1))
        def _(dt=dt):
            for db in (-1, 0, 1):
                coarse[1 + db, 1 + dt] = jnp.zeros((2 * rows, cols), f32)

    one_side = n_tile
    greeters = n_tile - 1
    greeters = greeters + jnp.where(band > 0, one_side, 0) + jnp.where(
        band < n_band - 1, one_side, 0
    )
    pl.semaphore_wait(barrier, greeters)

    def coarse_copy(db, dt):
        return pltpu.make_async_remote_copy(
            src_ref=coarse.at[1, 1],
            dst_ref=coarse.at[1 - db, 1 - dt],
            send_sem=c_send.at[1 + db, 1 + dt],
            recv_sem=c_recv.at[1 - db, 1 - dt],
            device_id=(band + db, tile + dt),
            device_id_type=MESH,
        )

    def coarse_in(db, dt):
        return pltpu.make_async_remote_copy(
            src_ref=coarse.at[1, 1],
            dst_ref=coarse.at[1 + db, 1 + dt],
            send_sem=c_send.at[1 - db, 1 - dt],
            recv_sem=c_recv.at[1 + db, 1 + dt],
            device_id=(band + db, tile + dt),
            device_id_type=MESH,
        )

    around = [(db, dt) for dt in (-1, 1, 0) for db in (-1, 0, 1) if (db, dt) != (0, 0)]

    def there(db, dt):
        ok = None
        for d, at, n in ((db, band, n_band), (dt, tile, n_tile)):
            if d:
                c = at > 0 if d < 0 else at < n - 1
                ok = c if ok is None else jnp.logical_and(ok, c)
        return ok

    for db, dt in around:
        when(there(db, dt), lambda db=db, dt=dt: coarse_copy(db, dt).start())

    def pair_copy(db, k):
        return pltpu.make_async_remote_copy(
            src_ref=pairs.at[1, tile],
            dst_ref=pairs.at[1 - db, tile],
            send_sem=p_send.at[1 + db, k],
            recv_sem=p_recv.at[1 - db, tile],
            device_id=device(db, k),
            device_id_type=MESH,
        )

    def pair_in(db, k):
        src = lax.rem(tile + k, n_tile)
        return pltpu.make_async_remote_copy(
            src_ref=pairs.at[1, tile],
            dst_ref=pairs.at[1 + db, src],
            send_sem=p_send.at[1 + db, k],
            recv_sem=p_recv.at[1 + db, src],
            device_id=device(db, k),
            device_id_type=MESH,
        )

    for db, k in partners:
        when(has_band[db], lambda db=db, k=k: pair_copy(db, k).start())

    full = n_tile * width
    scale = float(full * full) / 4.0 * entropy
    near_i = lax.broadcasted_iota(jnp.int32, (width, width), 0)
    near_j = lax.broadcasted_iota(jnp.int32, (width, width), 1)
    for t in range(n_tile):
        gap = ((t - tile) * width + near_i - near_j).astype(f32)
        mix[t] = jnp.exp(gap * gap * (-1.0 / scale))

    lanes = pair_ref.shape[1]
    base = (band - 1) * n_tile * tiles
    window = 3 * n_tile * tiles
    total = jnp.zeros((tiles, window), f32)
    for r in range(prow):
        src = pair_ref[r : r + 1, :]
        tgt = pair_ref[prow + r : prow + r + 1, :] - base
        a = jnp.where(
            lax.broadcasted_iota(jnp.int32, (tiles, lanes), 0) == src, 1.0, 0.0
        ).astype(jnp.bfloat16)
        b = jnp.where(
            lax.broadcasted_iota(jnp.int32, (window, lanes), 0) == tgt, 1.0, 0.0
        ).astype(jnp.bfloat16)
        total = total + lax.dot_general(a, b, NT, preferred_element_type=f32)
    lane = lax.broadcasted_iota(jnp.int32, (tiles, window), 1)
    own = lax.broadcasted_iota(jnp.int32, (tiles, window), 0)
    drow = (
        own + tiles - (lane // (n_tile * tiles)) * tiles - lane % tiles
    ).astype(f32)
    damp = drow * drow * (-1.0 / scale)
    count1[...] = total

    for db, dt in around:
        when(there(db, dt), lambda db=db, dt=dt: coarse_in(db, dt).wait_recv())

    span_r = rows + 2 * keep
    wide = 2 * cols
    grid_rows = n_band * rows
    for which in range(2):
        for db in (-1, 0, 1):
            lo = which * rows
            if db == -1:
                rs, rd = slice(lo + rows - keep, lo + rows), slice(0, keep)
            elif db == 0:
                rs, rd = slice(lo, lo + rows), slice(keep, keep + rows)
            else:
                rs, rd = slice(lo, lo + keep), slice(keep + rows, span_r)
            ext[which, rd, 0:cols] = coarse[1 + db, 1, rs]
            lane2 = lax.broadcasted_iota(jnp.int32, (keep if db else rows, cols), 1)
            ext[which, rd, cols:wide] = jnp.where(
                lane2 < cols // 2, coarse[1 + db, 2, rs], coarse[1 + db, 0, rs]
            )
    src_ext = ext[0]
    tgt_ext = ext[1]
    row_at = lax.broadcasted_iota(jnp.int32, (span_r, wide), 0) + band * rows - keep
    lane_at = lax.broadcasted_iota(jnp.int32, (span_r, wide), 1)
    col_at = jnp.where(lane_at < cols + cols // 2, lane_at, lane_at - wide) + tile * cols
    inside = jnp.logical_and(
        jnp.logical_and(row_at >= 0, row_at < grid_rows),
        jnp.logical_and(col_at >= 0, col_at < n_tile * cols),
    )

    def blur(field, lost):
        n = field.shape[0] - 2 * REACH
        across = taps[0] * field[0:n]
        for k in range(1, 2 * REACH + 1):
            across = across + taps[k] * field[k : k + n]
        result = taps[REACH] * across
        for k in range(1, REACH + 1):
            result = result + taps[REACH + k] * (
                pltpu.roll(across, k, 1) + pltpu.roll(across, wide - k, 1)
            )
        return result

    def power(x):
        return jnp.exp(coarse_power * jnp.log(x))

    def ones_blur(position, count):
        out = jnp.zeros(position.shape, f32)
        for k in range(-REACH, REACH + 1):
            at = position + k
            out = out + jnp.where(jnp.logical_and(at >= 0, at < count), taps[REACH + k], 0.0)
        return out

    edge_r = ones_blur(row_at[:, 0:1], grid_rows)
    edge_c = ones_blur(col_at[0:1, :], n_tile * cols)
    spread = edge_r * edge_c
    safe = jnp.where(inside, spread, 1.0)
    safe_src = jnp.where(inside, src_ext, 1.0)
    safe_tgt = jnp.where(inside, tgt_ext, 1.0)
    u = jnp.where(inside, power(safe_src / safe), 0.0)
    for lost in (4, 8, 12):
        field = u if lost == 4 else (v if lost == 8 else u)
        out = blur(field, lost)
        s = slice(lost, span_r - lost)
        mask = inside[s]
        mass = safe_src[s] if lost == 8 else safe_tgt[s]
        res = jnp.where(mask, power(mass / jnp.where(mask, out, 1.0)), 0.0)
        if lost == 8:
            u = res
        else:
            v = res
    u_ref[...] = u[keep - 8 : keep - 8 + rows, 0:cols]
    scaling_v = v[keep - 12 : keep - 12 + rows, 0:cols]
    v_ref[...] = scaling_v

    fold = tiles // rows
    log_v = jnp.log(scaling_v)
    parent = jnp.broadcast_to(log_v[:, None, :], (rows, fold, cols)).reshape(tiles, cols)
    field = (off_ref[...] + entropy * parent) / entropy + jnp.log(tm_ref[...])

    def gather(win, send, recv, value, between):
        win[1, tile] = value

        def over_tile(k):
            return pltpu.make_async_remote_copy(
                src_ref=win.at[1, tile],
                dst_ref=win.at[1, tile],
                send_sem=send.at[1, k],
                recv_sem=recv.at[1, tile],
                device_id=device(0, k),
                device_id_type=MESH,
            )

        def over_band(db, k):
            src = lax.rem(tile + k, n_tile)
            return pltpu.make_async_remote_copy(
                src_ref=win.at[1, src],
                dst_ref=win.at[1 - db, src],
                send_sem=send.at[1 + db, k],
                recv_sem=recv.at[1 - db, src],
                device_id=device(db, 0),
                device_id_type=MESH,
            )

        def arrive(db, k):
            src = lax.rem(tile + k, n_tile)
            return pltpu.make_async_remote_copy(
                src_ref=win.at[1, src],
                dst_ref=win.at[1 + db, src],
                send_sem=send.at[1 + db, k],
                recv_sem=recv.at[1 + db, src],
                device_id=device(db, 0) if db else device(0, k),
                device_id_type=MESH,
            )

        order = sorted(range(1, n_tile), key=lambda k: min(k, n_tile - k))
        for k in reversed(order):
            over_tile(k).start()
        for db in (-1, 1):
            when(has_band[db], lambda db=db: over_band(db, 0).start())
        between()
        for k in order:
            arrive(0, k).wait_recv()
            for db in (-1, 1):
                when(has_band[db], lambda db=db, k=k: over_band(db, k).start())
        for db in (-1, 1):

            def take(db=db):
                for k in [0] + order:
                    arrive(db, k).wait_recv()

            when(has_band[db], take)

        def finish():
            for k in order:
                over_tile(k).wait_send()
            for db in (-1, 1):

                def sent(db=db):
                    for k in range(n_tile):
                        over_band(db, k).wait_send()

                when(has_band[db], sent)

        return finish

    def reduce(win, count):
        values = win[...]
        flat = values.reshape(window, width)
        high = jnp.max(flat, axis=1, keepdims=True)
        near = jnp.exp(flat - high)
        blocks = near.reshape(3, n_tile, tiles, width)
        parts = [
            dot(blocks[:, t].reshape(3 * tiles, width), mix[t]).reshape(3, 1, tiles, width)
            for t in range(n_tile)
        ]
        spread = jnp.concatenate(parts, axis=1).reshape(window, width)
        high_row = column_to_row(high, window)
        n = count[...]
        lifted = jnp.where(n > 0.0, high_row + damp, -jnp.inf)
        peak = jnp.max(lifted, axis=1, keepdims=True)
        peak = jnp.where(peak == -jnp.inf, 0.0, peak)
        weight = n * jnp.exp(lifted - peak)
        summed = dot(weight, spread)
        return peak + jnp.log(summed)

    def incoming_counts():
        for db, k in partners:
            when(has_band[db], lambda db=db, k=k: pair_in(db, k).wait_recv())
        mine = (band * n_tile + tile) * tiles
        parts = []
        for b in range(3):
            for t in range(n_tile):
                here = pairs[b, t]
                part = jnp.zeros((tiles, tiles), f32)
                for r in range(prow):
                    src = here[r : r + 1]
                    tgt = here[prow + r : prow + r + 1] - mine
                    live = lax.broadcasted_iota(jnp.int32, (tiles, lanes), 0)
                    a = jnp.where(live == src, 1.0, 0.0).astype(jnp.bfloat16)
                    c = jnp.where(live == tgt, 1.0, 0.0).astype(jnp.bfloat16)
                    part = part + lax.dot_general(c, a, NT, preferred_element_type=f32)
                parts.append(part)
        count2[...] = jnp.concatenate(parts, axis=1)

    finish1 = gather(win1, w1_send, w1_recv, field, incoming_counts)
    potential = -damping * entropy * reduce(win1, count1)
    sp_ref[...] = potential
    eye = lax.broadcasted_iota(jnp.int32, (tiles, tiles), 0) == lax.broadcasted_iota(
        jnp.int32, (tiles, tiles), 1
    )
    cell_count = jnp.sum(jnp.where(eye, cnt_ref[...].astype(f32), 0.0), axis=1, keepdims=True)
    active = lax.broadcasted_iota(jnp.int32, (tiles, width), 1).astype(f32) < cell_count
    source_field = jnp.where(active, potential / entropy + jnp.log(sm_ref[...]), -jnp.inf)
    finish2 = gather(win2, w2_send, w2_recv, source_field, lambda: None)
    tp_ref[...] = -damping * entropy * reduce(win2, count2)

    for db, dt in around:
        when(there(db, dt), lambda db=db, dt=dt: coarse_copy(db, dt).wait_send())
    for db, k in partners:
        when(has_band[db], lambda db=db, k=k: pair_copy(db, k).wait_send())
    finish1()
    finish2()


def per_device(cs, ct, off, sm, tm, cnt, ps, pt):
    n_band = lax.axis_size("band")
    n_tile = lax.axis_size("tile")
    rows, cols = cs.shape
    tiles, width = off.shape
    pair = jnp.concatenate([ps.reshape(-1, 128), pt.reshape(-1, 128)], axis=0)
    f32 = jnp.float32
    window = 3 * n_tile * tiles
    dma = pltpu.SemaphoreType.DMA
    return pl.pallas_call(
        functools.partial(kernel, n_band, n_tile),
        out_shape=(
            jax.ShapeDtypeStruct((rows, cols), f32),
            jax.ShapeDtypeStruct((rows, cols), f32),
            jax.ShapeDtypeStruct((tiles, width), f32),
            jax.ShapeDtypeStruct((tiles, width), f32),
        ),
        in_specs=[pl.BlockSpec(memory_space=pltpu.VMEM)] * 7,
        out_specs=[pl.BlockSpec(memory_space=pltpu.VMEM)] * 4,
        scratch_shapes=[
            pltpu.VMEM((3, 3, 2 * rows, cols), f32),
            pltpu.VMEM((2, 3 * rows, 2 * cols), f32),
            pltpu.VMEM((3, n_tile) + pair.shape, jnp.int32),
            pltpu.VMEM((3, n_tile, tiles, width), f32),
            pltpu.VMEM((3, n_tile, tiles, width), f32),
            pltpu.VMEM((tiles, window), f32),
            pltpu.VMEM((tiles, window), f32),
            pltpu.VMEM((n_tile, width, width), f32),
            dma((3, 3)),
            dma((3, 3)),
            dma((3, n_tile)),
            dma((3, n_tile)),
            dma((3, n_tile)),
            dma((3, n_tile)),
            dma((3, n_tile)),
            dma((3, n_tile)),
        ],
        compiler_params=pltpu.CompilerParams(
            collective_id=0, has_side_effects=True, vmem_limit_bytes=32 * 1024 * 1024
        ),
    )(cs, ct, off, sm, tm, cnt.reshape(1, tiles), pair)


def solution(mesh):
    placed = (
        P("band", "tile"),
        P("band", "tile"),
        P(("band", "tile"), None),
        P(("band", "tile"), None),
        P(("band", "tile"), None),
        P(("band", "tile")),
        P(("band", "tile")),
        P(("band", "tile")),
    )
    return jax.shard_map(
        per_device,
        mesh=mesh,
        in_specs=placed,
        out_specs=(
            P("band", "tile"),
            P("band", "tile"),
            P(("band", "tile"), None),
            P(("band", "tile"), None),
        ),
        check_vma=False,
    )
```

```python
import functools
import math

import jax
import jax.numpy as jnp
from jax import lax
from jax.experimental import pallas as pl
from jax.experimental.pallas import tpu as pltpu
from jax.sharding import PartitionSpec as P

COARSE_ITERS = 2
REACH = 4
entropy = 0.5
damping = 0.8
coarse_power = 0.8
taps = [math.exp(-0.125 * k * k) for k in range(-REACH, REACH + 1)]
MESH = pl.DeviceIdType.MESH
NT = (((1,), (1,)), ((), ()))
NN = (((1,), (0,)), ((), ()))


def halves(x):
    high = x.astype(jnp.bfloat16)
    low = (x - high.astype(jnp.float32)).astype(jnp.bfloat16)
    return high, low


def column_to_row(col, tiles):
    out = []
    for at in range(0, tiles, 128):
        eye = lax.broadcasted_iota(jnp.int32, (128, 128), 0) == lax.broadcasted_iota(
            jnp.int32, (128, 128), 1
        )
        part = jnp.where(eye, col[at : at + 128], 0.0)
        out.append(jnp.sum(part, axis=0, keepdims=True))
    return jnp.concatenate(out, axis=1)


def kernel(
    n_band,
    n_tile,
    cs_ref,
    ct_ref,
    off_ref,
    sm_ref,
    tm_ref,
    cnt_ref,
    ps_ref,
    pt_ref,
    u_ref,
    v_ref,
    sp_ref,
    tp_ref,
    fine,
    cells,
    arrived,
    u_out,
    v_out,
    sp_out,
    tp_out,
    stored,
    coarse,
    side,
    edges,
    ext,
    pairs,
    win1,
    win2,
    count1,
    count2,
    mix,
    spread,
    peaks,
    c_send,
    c_recv,
    p_send,
    p_recv,
    w1_send,
    w1_recv,
    w2_send,
    w2_recv,
):
    rows, cols = cs_ref.shape
    tiles, width = off_ref.shape
    slots = ps_ref.shape[1]
    band = lax.axis_index("band")
    tile = lax.axis_index("tile")
    f32 = jnp.float32
    keep = rows

    barrier = pltpu.get_barrier_semaphore()
    has_band = {-1: band > 0, 0: True, 1: band < n_band - 1}

    def when(cond, body):
        if cond is True:
            body()
        else:
            pl.when(cond)(body)

    partners = [
        (db, k) for db in (-1, 0, 1) for k in range(n_tile) if (db, k) != (0, 0)
    ]

    def device(db, k):
        return (band + db, lax.rem(tile + k, n_tile))

    for db, k in partners:

        def greet(db=db, k=k):
            pl.semaphore_signal(barrier, inc=1, device_id=device(db, k), device_id_type=MESH)

        when(has_band[db], greet)

    loads = [
        pltpu.make_async_copy(src, dst, arrived.at[i])
        for i, (src, dst) in enumerate(
            (
                (cs_ref, coarse.at[1, 0]),
                (ct_ref, coarse.at[1, 1]),
                (ps_ref, pairs.at[1, tile, 0]),
                (pt_ref, pairs.at[1, tile, 1]),
                (off_ref, fine.at[0]),
                (tm_ref, fine.at[1]),
                (sm_ref, fine.at[2]),
                (cnt_ref, cells),
            )
        )
    ]
    for load in loads:
        load.start()
    stores = [
        pltpu.make_async_copy(src, dst, stored.at[i])
        for i, (src, dst) in enumerate(
            ((u_out, u_ref), (v_out, v_ref), (sp_out, sp_ref), (tp_out, tp_ref))
        )
    ]
    for db in (-1, 1):

        def blank(db=db):
            coarse[1 + db] = jnp.zeros((2, rows, cols), f32)
            for t in range(n_tile):
                pairs[1 + db, t] = jnp.full((2, 1, slots), -1, jnp.int32)
                win1[1 + db, t] = jnp.zeros((tiles, width), f32)
                win2[1 + db, t] = jnp.zeros((tiles, width), f32)
            for dt in range(2):
                side[1 + db, dt] = jnp.zeros((rows, cols), f32)

        pl.when(jnp.logical_not(has_band[db]))(blank)
    for dt in (-1, 1):
        here = tile + dt

        @pl.when(jnp.logical_or(here < 0, here > n_tile - 1))
        def _(dt=dt):
            for db in (-1, 0, 1):
                side[1 + db, (1 + dt) // 2] = jnp.zeros((rows, cols), f32)

    half = cols // 2
    edge_lane = lax.broadcasted_iota(jnp.int32, (rows, cols), 1)
    loads[0].wait()
    loads[1].wait()
    own_cs = coarse[1, 0]
    turned = pltpu.roll(coarse[1, 1], half, 1)
    edges[1] = jnp.where(edge_lane >= half, own_cs, turned)
    edges[0] = jnp.where(edge_lane < half, own_cs, turned)
    one_side = n_tile
    greeters = n_tile - 1
    greeters = greeters + jnp.where(band > 0, one_side, 0) + jnp.where(
        band < n_band - 1, one_side, 0
    )
    pl.semaphore_wait(barrier, greeters)

    def coarse_refs(db, dt):
        if dt == 0:
            return coarse.at[1], coarse.at[1 + db]
        return edges.at[(1 - dt) // 2], side.at[1 + db, (1 + dt) // 2]

    def coarse_copy(db, dt):
        return pltpu.make_async_remote_copy(
            src_ref=coarse_refs(-db, -dt)[0],
            dst_ref=coarse_refs(-db, -dt)[1],
            send_sem=c_send.at[1 + db, 1 + dt],
            recv_sem=c_recv.at[1 - db, 1 - dt],
            device_id=(band + db, tile + dt),
            device_id_type=MESH,
        )

    def coarse_in(db, dt):
        return pltpu.make_async_remote_copy(
            src_ref=coarse_refs(db, dt)[0],
            dst_ref=coarse_refs(db, dt)[1],
            send_sem=c_send.at[1 - db, 1 - dt],
            recv_sem=c_recv.at[1 + db, 1 + dt],
            device_id=(band + db, tile + dt),
            device_id_type=MESH,
        )

    around = [(db, dt) for dt in (-1, 1, 0) for db in (-1, 0, 1) if (db, dt) != (0, 0)]

    def there(db, dt):
        ok = None
        for d, at, n in ((db, band, n_band), (dt, tile, n_tile)):
            if d:
                c = at > 0 if d < 0 else at < n - 1
                ok = c if ok is None else jnp.logical_and(ok, c)
        return ok

    for db, dt in around:
        when(there(db, dt), lambda db=db, dt=dt: coarse_copy(db, dt).start())

    def pair_copy(db, k):
        return pltpu.make_async_remote_copy(
            src_ref=pairs.at[1, tile],
            dst_ref=pairs.at[1 - db, tile],
            send_sem=p_send.at[1 + db, k],
            recv_sem=p_recv.at[1 - db, tile],
            device_id=device(db, k),
            device_id_type=MESH,
        )

    def pair_in(db, k):
        src = lax.rem(tile + k, n_tile)
        return pltpu.make_async_remote_copy(
            src_ref=pairs.at[1, tile],
            dst_ref=pairs.at[1 + db, src],
            send_sem=p_send.at[1 + db, k],
            recv_sem=p_recv.at[1 + db, src],
            device_id=device(db, k),
            device_id_type=MESH,
        )

    loads[2].wait()
    loads[3].wait()
    for db, k in partners:
        when(has_band[db], lambda db=db, k=k: pair_copy(db, k).start())

    full = n_tile * width
    scale = float(full * full) / 4.0 * entropy
    near_i = lax.broadcasted_iota(jnp.int32, (width, width), 0)
    near_j = lax.broadcasted_iota(jnp.int32, (width, width), 1)
    mix_high, mix_low = halves(jnp.exp((near_i * near_j).astype(f32) * (2.0 / scale)))
    mix[0:width, 0:width] = mix_high
    mix[width : 2 * width, 0:width] = mix_high
    mix[0:width, width : 2 * width] = mix_low
    mix[width : 2 * width, width : 2 * width] = jnp.zeros((width, width), jnp.bfloat16)
    cell = lax.broadcasted_iota(jnp.int32, (1, width), 1)
    lift, ease = [], []
    for t in range(n_tile):
        gap = (t - tile) * width
        lift.append((-cell * cell - 2 * gap * cell).astype(f32) * (1.0 / scale))
        rest = (gap - cell).astype(f32)
        ease.append(jnp.exp(rest * rest * (-1.0 / scale)))

    base = (band - 1) * n_tile * tiles
    window = 3 * n_tile * tiles

    def hits(count, index):
        return jnp.where(
            lax.broadcasted_iota(jnp.int32, (count, slots), 0) == index, 1.0, 0.0
        ).astype(jnp.bfloat16)

    total = lax.dot_general(
        hits(tiles, pairs[1, tile, 0]),
        hits(window, pairs[1, tile, 1] - base),
        NT,
        preferred_element_type=f32,
    )
    lane = lax.broadcasted_iota(jnp.int32, (tiles, window), 1)
    own = lax.broadcasted_iota(jnp.int32, (tiles, window), 0)
    drow = (
        own + tiles - (lane // (n_tile * tiles)) * tiles - lane % tiles
    ).astype(f32)
    damp = drow * drow * (-1.0 / scale)
    count1[...] = total

    for db, dt in around:
        when(there(db, dt), lambda db=db, dt=dt: coarse_in(db, dt).wait_recv())

    span_r = rows + 2 * keep
    wide = 2 * cols
    grid_rows = n_band * rows
    for which in range(2):
        for db in (-1, 0, 1):
            lo = which * rows
            if db == -1:
                rs, rd = slice(lo + rows - keep, lo + rows), slice(0, keep)
            elif db == 0:
                rs, rd = slice(lo, lo + rows), slice(keep, keep + rows)
            else:
                rs, rd = slice(lo, lo + keep), slice(keep + rows, span_r)
            rs = slice(rs.start - lo, rs.stop - lo)
            ext[which, rd, 0:cols] = coarse[1 + db, which, rs]
            left, right = side[1 + db, 0, rs], side[1 + db, 1, rs]
            if which == 0:
                both = jnp.where(edge_lane < half, right, left)
            else:
                both = pltpu.roll(jnp.where(edge_lane < half, left, right), half, 1)
            ext[which, rd, cols:wide] = both
    src_ext = ext[0]
    tgt_ext = ext[1]
    row_at = lax.broadcasted_iota(jnp.int32, (span_r, wide), 0) + band * rows - keep
    lane_at = lax.broadcasted_iota(jnp.int32, (span_r, wide), 1)
    col_at = jnp.where(lane_at < cols + cols // 2, lane_at, lane_at - wide) + tile * cols
    inside = jnp.logical_and(
        jnp.logical_and(row_at >= 0, row_at < grid_rows),
        jnp.logical_and(col_at >= 0, col_at < n_tile * cols),
    )

    def blur(field, lost):
        n = field.shape[0] - 2 * REACH
        across = taps[0] * field[0:n]
        for k in range(1, 2 * REACH + 1):
            across = across + taps[k] * field[k : k + n]
        result = taps[REACH] * across
        for k in range(1, REACH + 1):
            result = result + taps[REACH + k] * (
                pltpu.roll(across, k, 1) + pltpu.roll(across, wide - k, 1)
            )
        return result

    def power(x):
        return jnp.exp(coarse_power * jnp.log(x))

    def ones_blur(position, count):
        out = jnp.zeros(position.shape, f32)
        for k in range(-REACH, REACH + 1):
            at = position + k
            out = out + jnp.where(jnp.logical_and(at >= 0, at < count), taps[REACH + k], 0.0)
        return out

    edge_r = ones_blur(row_at[:, 0:1], grid_rows)
    edge_c = ones_blur(col_at[0:1, :], n_tile * cols)
    safe = jnp.where(inside, edge_r * edge_c, 1.0)
    safe_src = jnp.where(inside, src_ext, 1.0)
    safe_tgt = jnp.where(inside, tgt_ext, 1.0)
    u = jnp.where(inside, power(safe_src / safe), 0.0)
    for lost in (4, 8, 12):
        field = u if lost == 4 else (v if lost == 8 else u)
        out = blur(field, lost)
        s = slice(lost, span_r - lost)
        mask = inside[s]
        mass = safe_src[s] if lost == 8 else safe_tgt[s]
        res = jnp.where(mask, power(mass / jnp.where(mask, out, 1.0)), 0.0)
        if lost == 8:
            u = res
        else:
            v = res
    u_out[...] = u[keep - 8 : keep - 8 + rows, 0:cols]
    scaling_v = v[keep - 12 : keep - 12 + rows, 0:cols]
    v_out[...] = scaling_v
    stores[0].start()
    stores[1].start()

    fold = tiles // rows
    log_v = jnp.log(scaling_v)
    parent = jnp.broadcast_to(log_v[:, None, :], (rows, fold, cols)).reshape(tiles, cols)
    for load in loads[4:]:
        load.wait()
    field = (fine[0] + entropy * parent) / entropy + jnp.log(fine[1])

    def gather(win, send, recv, value, between, absorb):
        win[1, tile] = value

        def over_tile(k):
            return pltpu.make_async_remote_copy(
                src_ref=win.at[1, tile],
                dst_ref=win.at[1, tile],
                send_sem=send.at[1, k],
                recv_sem=recv.at[1, tile],
                device_id=device(0, k),
                device_id_type=MESH,
            )

        def over_band(db, k):
            src = lax.rem(tile + k, n_tile)
            return pltpu.make_async_remote_copy(
                src_ref=win.at[1, src],
                dst_ref=win.at[1 - db, src],
                send_sem=send.at[1 + db, k],
                recv_sem=recv.at[1 - db, src],
                device_id=device(db, 0),
                device_id_type=MESH,
            )

        def arrive(db, k):
            src = lax.rem(tile + k, n_tile)
            return pltpu.make_async_remote_copy(
                src_ref=win.at[1, src],
                dst_ref=win.at[1 + db, src],
                send_sem=send.at[1 + db, k],
                recv_sem=recv.at[1 + db, src],
                device_id=device(db, 0) if db else device(0, k),
                device_id_type=MESH,
            )

        order = sorted(range(1, n_tile), key=lambda k: min(k, n_tile - k))
        for k in reversed(order):
            over_tile(k).start()
        for db in (-1, 1):
            when(has_band[db], lambda db=db: over_band(db, 0).start())
        between()
        for k in order:
            arrive(0, k).wait_recv()
            for db in (-1, 1):
                when(has_band[db], lambda db=db, k=k: over_band(db, k).start())
        absorb(1)
        for db in (-1, 1):

            def take(db=db):
                for k in [0] + order:
                    arrive(db, k).wait_recv()

            when(has_band[db], take)
            absorb(1 + db)

        def finish():
            for k in order:
                over_tile(k).wait_send()
            for db in (-1, 1):

                def sent(db=db):
                    for k in range(n_tile):
                        over_band(db, k).wait_send()

                when(has_band[db], sent)

        return finish

    per_band = n_tile * tiles

    def absorber(win):
        def absorb(b):
            lifted = jnp.concatenate([win[b, t] + lift[t] for t in range(n_tile)], axis=0)
            high = jnp.max(lifted, axis=1, keepdims=True)
            near = jnp.concatenate(halves(jnp.exp(lifted - high)), axis=1)
            out = lax.dot_general(near, mix[...], NN, preferred_element_type=f32)
            out = out[:, 0:width] + out[:, width : 2 * width]
            for t in range(n_tile):
                part = out[t * tiles : (t + 1) * tiles] * ease[t]
                part_high, part_low = halves(part)
                rows_at = slice(b * per_band + t * tiles, b * per_band + (t + 1) * tiles)
                spread[rows_at, 0:width] = part_high
                spread[rows_at, width : 2 * width] = part_low
            peaks[:, b * per_band : (b + 1) * per_band] = column_to_row(high, per_band)

        return absorb

    def reduce(count):
        n = count[...]
        lifted = jnp.where(n > 0.0, peaks[...] + damp, -jnp.inf)
        peak = jnp.max(lifted, axis=1, keepdims=True)
        weight = n * jnp.exp(lifted - peak)
        both = jnp.concatenate(halves(weight), axis=0)
        out = lax.dot_general(both, spread[...], NN, preferred_element_type=f32)
        summed = out[0:tiles, 0:width] + (
            out[tiles : 2 * tiles, 0:width] + out[0:tiles, width : 2 * width]
        )
        return peak + jnp.log(summed)

    mine = (band * n_tile + tile) * tiles

    def counts_of(b, t):
        at = (b * n_tile + t) * tiles
        count2[:, at : at + tiles] = lax.dot_general(
            hits(tiles, pairs[b, t, 1] - mine),
            hits(tiles, pairs[b, t, 0]),
            NT,
            preferred_element_type=f32,
        )

    blocks = [(b, t) for b in range(3) for t in range(n_tile)]

    def early_counts():
        for db, k in partners:
            when(has_band[db], lambda db=db, k=k: pair_in(db, k).wait_recv())
        for b, t in blocks[0 : len(blocks) // 2]:
            counts_of(b, t)

    def late_counts():
        for b, t in blocks[len(blocks) // 2 :]:
            counts_of(b, t)

    finish1 = gather(win1, w1_send, w1_recv, field, early_counts, absorber(win1))
    potential = -damping * entropy * reduce(count1)
    sp_out[...] = potential
    eye = lax.broadcasted_iota(jnp.int32, (tiles, tiles), 0) == lax.broadcasted_iota(
        jnp.int32, (tiles, tiles), 1
    )
    cell_count = jnp.sum(jnp.where(eye, cells[...].astype(f32), 0.0), axis=1, keepdims=True)
    active = lax.broadcasted_iota(jnp.int32, (tiles, width), 1).astype(f32) < cell_count
    source_field = jnp.where(active, potential / entropy + jnp.log(fine[2]), -jnp.inf)
    finish2 = gather(
        win2, w2_send, w2_recv, source_field, late_counts, absorber(win2)
    )
    stores[2].start()
    tp_out[...] = -damping * entropy * reduce(count2)
    stores[3].start()

    for db, dt in around:
        when(there(db, dt), lambda db=db, dt=dt: coarse_copy(db, dt).wait_send())
    for db, k in partners:
        when(has_band[db], lambda db=db, k=k: pair_copy(db, k).wait_send())
    finish1()
    finish2()
    for store in stores:
        store.wait()


def write_out(*refs):
    sources, targets, sems = refs[0:4], refs[4:8], refs[8]
    copies = [pltpu.make_async_copy(sources[i], targets[i], sems.at[i]) for i in range(4)]
    for copy in copies:
        copy.start()
    for copy in copies:
        copy.wait()


def per_device(cs, ct, off, sm, tm, cnt, ps, pt):
    n_band = lax.axis_size("band")
    n_tile = lax.axis_size("tile")
    rows, cols = cs.shape
    tiles, width = off.shape
    f32 = jnp.float32
    slots = ps.shape[0]
    window = 3 * n_tile * tiles
    dma = pltpu.SemaphoreType.DMA
    shapes = (
        jax.ShapeDtypeStruct((rows, cols), f32),
        jax.ShapeDtypeStruct((rows, cols), f32),
        jax.ShapeDtypeStruct((tiles, width), f32),
        jax.ShapeDtypeStruct((tiles, width), f32),
    )
    results = pl.pallas_call(
        functools.partial(kernel, n_band, n_tile),
        out_shape=shapes,
        in_specs=[pl.BlockSpec(memory_space=pltpu.HBM)] * 8,
        out_specs=[pl.BlockSpec(memory_space=pltpu.HBM)] * 4,
        scratch_shapes=[
            pltpu.VMEM((3, tiles, width), f32),
            pltpu.VMEM((1, tiles), jnp.int32),
            dma((8,)),
            pltpu.VMEM((rows, cols), f32),
            pltpu.VMEM((rows, cols), f32),
            pltpu.VMEM((tiles, width), f32),
            pltpu.VMEM((tiles, width), f32),
            dma((4,)),
            pltpu.VMEM((3, 2, rows, cols), f32),
            pltpu.VMEM((3, 2, rows, cols), f32),
            pltpu.VMEM((2, rows, cols), f32),
            pltpu.VMEM((2, 3 * rows, 2 * cols), f32),
            pltpu.VMEM((3, n_tile, 2, 1, slots), jnp.int32),
            pltpu.VMEM((3, n_tile, tiles, width), f32),
            pltpu.VMEM((3, n_tile, tiles, width), f32),
            pltpu.VMEM((tiles, window), f32),
            pltpu.VMEM((tiles, window), f32),
            pltpu.VMEM((2 * width, 2 * width), jnp.bfloat16),
            pltpu.VMEM((window, 2 * width), jnp.bfloat16),
            pltpu.VMEM((1, window), f32),
            dma((3, 3)),
            dma((3, 3)),
            dma((3, n_tile)),
            dma((3, n_tile)),
            dma((3, n_tile)),
            dma((3, n_tile)),
            dma((3, n_tile)),
            dma((3, n_tile)),
        ],
        compiler_params=pltpu.CompilerParams(
            collective_id=0, has_side_effects=True, vmem_limit_bytes=60 * 1024 * 1024
        ),
    )(cs, ct, off, sm, tm, cnt.reshape(1, tiles), ps.reshape(1, slots), pt.reshape(1, slots))
    return pl.pallas_call(
        write_out,
        out_shape=shapes,
        in_specs=[pl.BlockSpec(memory_space=pltpu.HBM)] * 4,
        out_specs=[pl.BlockSpec(memory_space=pltpu.HBM)] * 4,
        scratch_shapes=[dma((4,))],
        compiler_params=pltpu.CompilerParams(vmem_limit_bytes=60 * 1024 * 1024),
    )(*results)


def solution(mesh):
    placed = (
        P("band", "tile"),
        P("band", "tile"),
        P(("band", "tile"), None),
        P(("band", "tile"), None),
        P(("band", "tile"), None),
        P(("band", "tile")),
        P(("band", "tile")),
        P(("band", "tile")),
    )
    return jax.shard_map(
        per_device,
        mesh=mesh,
        in_specs=placed,
        out_specs=(
            P("band", "tile"),
            P("band", "tile"),
            P(("band", "tile"), None),
            P(("band", "tile"), None),
        ),
        check_vma=False,
    )
```

```python
import functools
import math

import jax
import jax.numpy as jnp
from jax import lax
from jax.experimental import pallas as pl
from jax.experimental.pallas import tpu as pltpu
from jax.sharding import PartitionSpec as P

COARSE_ITERS = 2
REACH = 4
entropy = 0.5
damping = 0.8
coarse_power = 0.8
taps = [math.exp(-0.125 * k * k) for k in range(-REACH, REACH + 1)]
MESH = pl.DeviceIdType.MESH
NT = (((1,), (1,)), ((), ()))
NN = (((1,), (0,)), ((), ()))


def halves(x):
    high = x.astype(jnp.bfloat16)
    low = (x - high.astype(jnp.float32)).astype(jnp.bfloat16)
    return high, low


def column_to_row(col, tiles):
    out = []
    for at in range(0, tiles, 128):
        eye = lax.broadcasted_iota(jnp.int32, (128, 128), 0) == lax.broadcasted_iota(
            jnp.int32, (128, 128), 1
        )
        part = jnp.where(eye, col[at : at + 128], 0.0)
        out.append(jnp.sum(part, axis=0, keepdims=True))
    return jnp.concatenate(out, axis=1)


def kernel(
    n_band,
    n_tile,
    cs_ref,
    ct_ref,
    off_ref,
    sm_ref,
    tm_ref,
    cnt_ref,
    ps_ref,
    pt_ref,
    out_ref,
    fine,
    cells,
    arrived,
    u_out,
    v_out,
    sp_out,
    tp_out,
    stored,
    coarse,
    side,
    edges,
    ext,
    pairs,
    win1,
    win2,
    count1,
    count2,
    mix,
    spread,
    peaks,
    c_send,
    c_recv,
    p_send,
    p_recv,
    w1_send,
    w1_recv,
    w2_send,
    w2_recv,
):
    rows, cols = cs_ref.shape
    tiles, width = off_ref.shape
    slots = ps_ref.shape[1]
    band = lax.axis_index("band")
    tile = lax.axis_index("tile")
    f32 = jnp.float32
    keep = rows

    barrier = pltpu.get_barrier_semaphore()
    has_band = {-1: band > 0, 0: True, 1: band < n_band - 1}

    odd = lax.rem(band, 2) == 1
    paired = {
        -1: jnp.logical_and(has_band[-1], odd),
        1: jnp.logical_and(has_band[1], jnp.logical_not(odd)),
    }
    apart = {
        -1: jnp.logical_and(has_band[-1], jnp.logical_not(odd)),
        1: jnp.logical_and(has_band[1], odd),
    }

    def when(cond, body):
        if cond is True:
            body()
        else:
            pl.when(cond)(body)

    partners = [
        (db, k) for db in (-1, 0, 1) for k in range(n_tile) if (db, k) != (0, 0)
    ]

    def device(db, k):
        return (band + db, lax.rem(tile + k, n_tile))

    for db, k in partners:

        def greet(db=db, k=k):
            pl.semaphore_signal(barrier, inc=1, device_id=device(db, k), device_id_type=MESH)

        when(has_band[db], greet)

    loads = [
        pltpu.make_async_copy(src, dst, arrived.at[i])
        for i, (src, dst) in enumerate(
            (
                (cs_ref, coarse.at[1, 0]),
                (ct_ref, coarse.at[1, 1]),
                (ps_ref, pairs.at[1, tile, 0]),
                (pt_ref, pairs.at[1, tile, 1]),
                (off_ref, fine.at[0]),
                (tm_ref, fine.at[1]),
                (sm_ref, fine.at[2]),
                (cnt_ref, cells),
            )
        )
    ]
    for load in loads:
        load.start()
    stores = [
        pltpu.make_async_copy(src, dst, stored.at[i])
        for i, (src, dst) in enumerate(
            (
                (u_out, out_ref.at[0:rows]),
                (v_out, out_ref.at[rows : 2 * rows]),
                (sp_out, out_ref.at[2 * rows : 2 * rows + tiles]),
                (tp_out, out_ref.at[2 * rows + tiles : 2 * rows + 2 * tiles]),
            )
        )
    ]
    for db in (-1, 1):

        def blank(db=db):
            coarse[1 + db] = jnp.zeros((2, rows, cols), f32)
            for t in range(n_tile):
                pairs[1 + db, t] = jnp.full((2, 1, slots), -1, jnp.int32)
                win1[1 + db, t] = jnp.zeros((tiles, width), f32)
                win2[1 + db, t] = jnp.zeros((tiles, width), f32)
            for dt in range(2):
                side[1 + db, dt] = jnp.zeros((rows, cols), f32)

        pl.when(jnp.logical_not(has_band[db]))(blank)
    for dt in (-1, 1):
        here = tile + dt

        @pl.when(jnp.logical_or(here < 0, here > n_tile - 1))
        def _(dt=dt):
            for db in (-1, 0, 1):
                side[1 + db, (1 + dt) // 2] = jnp.zeros((rows, cols), f32)

    half = cols // 2
    edge_lane = lax.broadcasted_iota(jnp.int32, (rows, cols), 1)
    loads[0].wait()
    loads[1].wait()
    own_cs = coarse[1, 0]
    turned = pltpu.roll(coarse[1, 1], half, 1)
    edges[1] = jnp.where(edge_lane >= half, own_cs, turned)
    edges[0] = jnp.where(edge_lane < half, own_cs, turned)
    one_side = n_tile
    greeters = n_tile - 1
    greeters = greeters + jnp.where(band > 0, one_side, 0) + jnp.where(
        band < n_band - 1, one_side, 0
    )
    pl.semaphore_wait(barrier, greeters)

    def coarse_refs(db, dt):
        if dt == 0:
            return coarse.at[1], coarse.at[1 + db]
        return edges.at[(1 - dt) // 2], side.at[1 + db, (1 + dt) // 2]

    def coarse_copy(db, dt):
        return pltpu.make_async_remote_copy(
            src_ref=coarse_refs(-db, -dt)[0],
            dst_ref=coarse_refs(-db, -dt)[1],
            send_sem=c_send.at[1 + db, 1 + dt],
            recv_sem=c_recv.at[1 - db, 1 - dt],
            device_id=(band + db, tile + dt),
            device_id_type=MESH,
        )

    def coarse_in(db, dt):
        return pltpu.make_async_remote_copy(
            src_ref=coarse_refs(db, dt)[0],
            dst_ref=coarse_refs(db, dt)[1],
            send_sem=c_send.at[1 - db, 1 - dt],
            recv_sem=c_recv.at[1 + db, 1 + dt],
            device_id=(band + db, tile + dt),
            device_id_type=MESH,
        )

    around = [(db, dt) for dt in (-1, 1, 0) for db in (-1, 0, 1) if (db, dt) != (0, 0)]

    def there(db, dt):
        ok = None
        for d, at, n in ((db, band, n_band), (dt, tile, n_tile)):
            if d:
                c = at > 0 if d < 0 else at < n - 1
                ok = c if ok is None else jnp.logical_and(ok, c)
        return ok

    for db, dt in around:
        when(there(db, dt), lambda db=db, dt=dt: coarse_copy(db, dt).start())

    def pair_copy(db, k):
        return pltpu.make_async_remote_copy(
            src_ref=pairs.at[1, tile],
            dst_ref=pairs.at[1 - db, tile],
            send_sem=p_send.at[1 + db, k],
            recv_sem=p_recv.at[1 - db, tile],
            device_id=device(db, k),
            device_id_type=MESH,
        )

    def pair_in(db, k):
        src = lax.rem(tile + k, n_tile)
        return pltpu.make_async_remote_copy(
            src_ref=pairs.at[1, tile],
            dst_ref=pairs.at[1 + db, src],
            send_sem=p_send.at[1 + db, k],
            recv_sem=p_recv.at[1 + db, src],
            device_id=device(db, k),
            device_id_type=MESH,
        )

    loads[2].wait()
    loads[3].wait()
    for db, k in partners:
        when(has_band[db], lambda db=db, k=k: pair_copy(db, k).start())

    full = n_tile * width
    scale = float(full * full) / 4.0 * entropy
    near_i = lax.broadcasted_iota(jnp.int32, (width, width), 0)
    near_j = lax.broadcasted_iota(jnp.int32, (width, width), 1)
    mix_high, mix_low = halves(jnp.exp((near_i * near_j).astype(f32) * (2.0 / scale)))
    mix[0:width, 0:width] = mix_high
    mix[width : 2 * width, 0:width] = mix_high
    mix[0:width, width : 2 * width] = mix_low
    mix[width : 2 * width, width : 2 * width] = jnp.zeros((width, width), jnp.bfloat16)
    cell = lax.broadcasted_iota(jnp.int32, (1, width), 1)
    lift, ease = [], []
    for t in range(n_tile):
        gap = (t - tile) * width
        lift.append((-cell * cell - 2 * gap * cell).astype(f32) * (1.0 / scale))
        rest = (gap - cell).astype(f32)
        ease.append(jnp.exp(rest * rest * (-1.0 / scale)))

    base = (band - 1) * n_tile * tiles
    window = 3 * n_tile * tiles

    def hits(count, index):
        return jnp.where(
            lax.broadcasted_iota(jnp.int32, (count, slots), 0) == index, 1.0, 0.0
        ).astype(jnp.bfloat16)

    total = lax.dot_general(
        hits(tiles, pairs[1, tile, 0]),
        hits(window, pairs[1, tile, 1] - base),
        NT,
        preferred_element_type=f32,
    )
    lane = lax.broadcasted_iota(jnp.int32, (tiles, window), 1)
    own = lax.broadcasted_iota(jnp.int32, (tiles, window), 0)
    drow = (
        own + tiles - (lane // (n_tile * tiles)) * tiles - lane % tiles
    ).astype(f32)
    damp = drow * drow * (-1.0 / scale)
    count1[...] = total

    for db, dt in around:
        when(there(db, dt), lambda db=db, dt=dt: coarse_in(db, dt).wait_recv())

    span_r = rows + 2 * keep
    wide = 2 * cols
    grid_rows = n_band * rows
    for which in range(2):
        for db in (-1, 0, 1):
            lo = which * rows
            if db == -1:
                rs, rd = slice(lo + rows - keep, lo + rows), slice(0, keep)
            elif db == 0:
                rs, rd = slice(lo, lo + rows), slice(keep, keep + rows)
            else:
                rs, rd = slice(lo, lo + keep), slice(keep + rows, span_r)
            rs = slice(rs.start - lo, rs.stop - lo)
            ext[which, rd, 0:cols] = coarse[1 + db, which, rs]
            left, right = side[1 + db, 0, rs], side[1 + db, 1, rs]
            if which == 0:
                both = jnp.where(edge_lane < half, right, left)
            else:
                both = pltpu.roll(jnp.where(edge_lane < half, left, right), half, 1)
            ext[which, rd, cols:wide] = both
    src_ext = ext[0]
    tgt_ext = ext[1]
    row_at = lax.broadcasted_iota(jnp.int32, (span_r, wide), 0) + band * rows - keep
    lane_at = lax.broadcasted_iota(jnp.int32, (span_r, wide), 1)
    col_at = jnp.where(lane_at < cols + cols // 2, lane_at, lane_at - wide) + tile * cols
    inside = jnp.logical_and(
        jnp.logical_and(row_at >= 0, row_at < grid_rows),
        jnp.logical_and(col_at >= 0, col_at < n_tile * cols),
    )

    def blur(field, lost):
        n = field.shape[0] - 2 * REACH
        across = taps[0] * field[0:n]
        for k in range(1, 2 * REACH + 1):
            across = across + taps[k] * field[k : k + n]
        result = taps[REACH] * across
        for k in range(1, REACH + 1):
            result = result + taps[REACH + k] * (
                pltpu.roll(across, k, 1) + pltpu.roll(across, wide - k, 1)
            )
        return result

    def power(x):
        return jnp.exp(coarse_power * jnp.log(x))

    def ones_blur(position, count):
        out = jnp.zeros(position.shape, f32)
        for k in range(-REACH, REACH + 1):
            at = position + k
            out = out + jnp.where(jnp.logical_and(at >= 0, at < count), taps[REACH + k], 0.0)
        return out

    edge_r = ones_blur(row_at[:, 0:1], grid_rows)
    edge_c = ones_blur(col_at[0:1, :], n_tile * cols)
    safe = jnp.where(inside, edge_r * edge_c, 1.0)
    safe_src = jnp.where(inside, src_ext, 1.0)
    safe_tgt = jnp.where(inside, tgt_ext, 1.0)
    u = jnp.where(inside, power(safe_src / safe), 0.0)
    for lost in (4, 8, 12):
        field = u if lost == 4 else (v if lost == 8 else u)
        out = blur(field, lost)
        s = slice(lost, span_r - lost)
        mask = inside[s]
        mass = safe_src[s] if lost == 8 else safe_tgt[s]
        res = jnp.where(mask, power(mass / jnp.where(mask, out, 1.0)), 0.0)
        if lost == 8:
            u = res
        else:
            v = res
    u_out[...] = u[keep - 8 : keep - 8 + rows, 0:cols]
    scaling_v = v[keep - 12 : keep - 12 + rows, 0:cols]
    v_out[...] = scaling_v
    stores[0].start()
    stores[1].start()

    fold = tiles // rows
    log_v = jnp.log(scaling_v)
    parent = jnp.broadcast_to(log_v[:, None, :], (rows, fold, cols)).reshape(tiles, cols)
    for load in loads[4:]:
        load.wait()
    field = (fine[0] + entropy * parent) / entropy + jnp.log(fine[1])

    def gather(win, send, recv, value, between, absorb):
        win[1, tile] = value

        def outward(db, k):
            return pltpu.make_async_remote_copy(
                src_ref=win.at[1, tile],
                dst_ref=win.at[1 - db, tile],
                send_sem=send.at[1 + db, k],
                recv_sem=recv.at[1 - db, tile],
                device_id=device(db, k),
                device_id_type=MESH,
            )

        def onward(db, k):
            src = lax.rem(tile + k, n_tile)
            return pltpu.make_async_remote_copy(
                src_ref=win.at[1, src],
                dst_ref=win.at[1 - db, src],
                send_sem=send.at[1 + db, k],
                recv_sem=recv.at[1 - db, src],
                device_id=device(db, 0),
                device_id_type=MESH,
            )

        def arrive(db, k):
            src = lax.rem(tile + k, n_tile)
            return pltpu.make_async_remote_copy(
                src_ref=win.at[1, tile],
                dst_ref=win.at[1 + db, src],
                send_sem=send.at[1 + db, k],
                recv_sem=recv.at[1 + db, src],
                device_id=device(db, k),
                device_id_type=MESH,
            )

        order = sorted(range(1, n_tile), key=lambda k: min(k, n_tile - k))
        for k in reversed(order):
            outward(0, k).start()
        for k in list(reversed(order)) + [0]:
            for db in (-1, 1):
                go = apart[db] if k else has_band[db]
                when(go, lambda db=db, k=k: outward(db, k).start())
        for k in order:
            arrive(0, k).wait_recv()
            for db in (-1, 1):
                when(paired[db], lambda db=db, k=k: onward(db, k).start())
        between()
        absorb(1)
        for db in (-1, 1):

            def take(db=db):
                for k in [0] + order:
                    arrive(db, k).wait_recv()

            when(has_band[db], take)
            absorb(1 + db)

        def finish():
            for db, k in partners:
                go = apart[db] if db and k else has_band[db]
                when(go, lambda db=db, k=k: outward(db, k).wait_send())
                if db and k:
                    when(paired[db], lambda db=db, k=k: onward(db, k).wait_send())

        return finish

    per_band = n_tile * tiles

    def absorber(win):
        def absorb(b):
            lifted = jnp.concatenate([win[b, t] + lift[t] for t in range(n_tile)], axis=0)
            high = jnp.max(lifted, axis=1, keepdims=True)
            near = jnp.concatenate(halves(jnp.exp(lifted - high)), axis=1)
            out = lax.dot_general(near, mix[...], NN, preferred_element_type=f32)
            out = out[:, 0:width] + out[:, width : 2 * width]
            for t in range(n_tile):
                part = out[t * tiles : (t + 1) * tiles] * ease[t]
                part_high, part_low = halves(part)
                rows_at = slice(b * per_band + t * tiles, b * per_band + (t + 1) * tiles)
                spread[rows_at, 0:width] = part_high
                spread[rows_at, width : 2 * width] = part_low
            peaks[:, b * per_band : (b + 1) * per_band] = column_to_row(high, per_band)

        return absorb

    def reduce(count):
        n = count[...]
        lifted = jnp.where(n > 0.0, peaks[...] + damp, -jnp.inf)
        peak = jnp.max(lifted, axis=1, keepdims=True)
        weight = n * jnp.exp(lifted - peak)
        both = jnp.concatenate(halves(weight), axis=0)
        out = lax.dot_general(both, spread[...], NN, preferred_element_type=f32)
        summed = out[0:tiles, 0:width] + (
            out[tiles : 2 * tiles, 0:width] + out[0:tiles, width : 2 * width]
        )
        return peak + jnp.log(summed)

    mine = (band * n_tile + tile) * tiles

    def counts_of(b, t):
        at = (b * n_tile + t) * tiles
        count2[:, at : at + tiles] = lax.dot_general(
            hits(tiles, pairs[b, t, 1] - mine),
            hits(tiles, pairs[b, t, 0]),
            NT,
            preferred_element_type=f32,
        )

    blocks = [(b, t) for b in range(3) for t in range(n_tile)]

    def early_counts():
        for db, k in partners:
            when(has_band[db], lambda db=db, k=k: pair_in(db, k).wait_recv())
        for b, t in blocks[0 : len(blocks) // 2]:
            counts_of(b, t)

    def late_counts():
        for b, t in blocks[len(blocks) // 2 :]:
            counts_of(b, t)

    finish1 = gather(win1, w1_send, w1_recv, field, early_counts, absorber(win1))
    potential = -damping * entropy * reduce(count1)
    sp_out[...] = potential
    eye = lax.broadcasted_iota(jnp.int32, (tiles, tiles), 0) == lax.broadcasted_iota(
        jnp.int32, (tiles, tiles), 1
    )
    cell_count = jnp.sum(jnp.where(eye, cells[...].astype(f32), 0.0), axis=1, keepdims=True)
    active = lax.broadcasted_iota(jnp.int32, (tiles, width), 1).astype(f32) < cell_count
    source_field = jnp.where(active, potential / entropy + jnp.log(fine[2]), -jnp.inf)
    finish2 = gather(
        win2, w2_send, w2_recv, source_field, late_counts, absorber(win2)
    )
    stores[2].start()
    tp_out[...] = -damping * entropy * reduce(count2)
    stores[3].start()

    for db, dt in around:
        when(there(db, dt), lambda db=db, dt=dt: coarse_copy(db, dt).wait_send())
    for db, k in partners:
        when(has_band[db], lambda db=db, k=k: pair_copy(db, k).wait_send())
    finish1()
    finish2()
    for store in stores:
        store.wait()


def write_out(packed, *outs):
    at = 0
    for out in outs:
        count = out.shape[0]
        out[...] = packed[at : at + count]
        at += count


def per_device(cs, ct, off, sm, tm, cnt, ps, pt):
    n_band = lax.axis_size("band")
    n_tile = lax.axis_size("tile")
    rows, cols = cs.shape
    tiles, width = off.shape
    f32 = jnp.float32
    slots = ps.shape[0]
    window = 3 * n_tile * tiles
    dma = pltpu.SemaphoreType.DMA
    shapes = (
        jax.ShapeDtypeStruct((rows, cols), f32),
        jax.ShapeDtypeStruct((rows, cols), f32),
        jax.ShapeDtypeStruct((tiles, width), f32),
        jax.ShapeDtypeStruct((tiles, width), f32),
    )
    packed = pl.pallas_call(
        functools.partial(kernel, n_band, n_tile),
        out_shape=jax.ShapeDtypeStruct((2 * rows + 2 * tiles, width), f32),
        in_specs=[pl.BlockSpec(memory_space=pltpu.HBM)] * 8,
        out_specs=pl.BlockSpec(memory_space=pltpu.HBM),
        scratch_shapes=[
            pltpu.VMEM((3, tiles, width), f32),
            pltpu.VMEM((1, tiles), jnp.int32),
            dma((8,)),
            pltpu.VMEM((rows, cols), f32),
            pltpu.VMEM((rows, cols), f32),
            pltpu.VMEM((tiles, width), f32),
            pltpu.VMEM((tiles, width), f32),
            dma((4,)),
            pltpu.VMEM((3, 2, rows, cols), f32),
            pltpu.VMEM((3, 2, rows, cols), f32),
            pltpu.VMEM((2, rows, cols), f32),
            pltpu.VMEM((2, 3 * rows, 2 * cols), f32),
            pltpu.VMEM((3, n_tile, 2, 1, slots), jnp.int32),
            pltpu.VMEM((3, n_tile, tiles, width), f32),
            pltpu.VMEM((3, n_tile, tiles, width), f32),
            pltpu.VMEM((tiles, window), f32),
            pltpu.VMEM((tiles, window), f32),
            pltpu.VMEM((2 * width, 2 * width), jnp.bfloat16),
            pltpu.VMEM((window, 2 * width), jnp.bfloat16),
            pltpu.VMEM((1, window), f32),
            dma((3, 3)),
            dma((3, 3)),
            dma((3, n_tile)),
            dma((3, n_tile)),
            dma((3, n_tile)),
            dma((3, n_tile)),
            dma((3, n_tile)),
            dma((3, n_tile)),
        ],
        compiler_params=pltpu.CompilerParams(
            collective_id=0, has_side_effects=True, vmem_limit_bytes=60 * 1024 * 1024
        ),
    )(cs, ct, off, sm, tm, cnt.reshape(1, tiles), ps.reshape(1, slots), pt.reshape(1, slots))
    return pl.pallas_call(
        write_out,
        out_shape=shapes,
        compiler_params=pltpu.CompilerParams(vmem_limit_bytes=60 * 1024 * 1024),
    )(packed)


def solution(mesh):
    placed = (
        P("band", "tile"),
        P("band", "tile"),
        P(("band", "tile"), None),
        P(("band", "tile"), None),
        P(("band", "tile"), None),
        P(("band", "tile")),
        P(("band", "tile")),
        P(("band", "tile")),
    )
    return jax.shard_map(
        per_device,
        mesh=mesh,
        in_specs=placed,
        out_specs=(
            P("band", "tile"),
            P("band", "tile"),
            P(("band", "tile"), None),
            P(("band", "tile"), None),
        ),
        check_vma=False,
    )
```

```python
import functools
import math

import jax
import jax.numpy as jnp
from jax import lax
from jax.experimental import pallas as pl
from jax.experimental.pallas import tpu as pltpu
from jax.sharding import PartitionSpec as P

COARSE_ITERS = 2
REACH = 4
entropy = 0.5
damping = 0.8
coarse_power = 0.8
taps = [math.exp(-0.125 * k * k) for k in range(-REACH, REACH + 1)]
MESH = pl.DeviceIdType.MESH
NT = (((1,), (1,)), ((), ()))
NN = (((1,), (0,)), ((), ()))


def halves(x):
    high = x.astype(jnp.bfloat16)
    low = (x - high.astype(jnp.float32)).astype(jnp.bfloat16)
    return high, low


def column_to_row(col, tiles):
    out = []
    for at in range(0, tiles, 128):
        eye = lax.broadcasted_iota(jnp.int32, (128, 128), 0) == lax.broadcasted_iota(
            jnp.int32, (128, 128), 1
        )
        part = jnp.where(eye, col[at : at + 128], 0.0)
        out.append(jnp.sum(part, axis=0, keepdims=True))
    return jnp.concatenate(out, axis=1)


def kernel(
    n_band,
    n_tile,
    cs_ref,
    ct_ref,
    off_ref,
    sm_ref,
    tm_ref,
    cnt_ref,
    ps_ref,
    pt_ref,
    out_ref,
    fine,
    cells,
    arrived,
    u_out,
    v_out,
    sp_out,
    tp_out,
    stored,
    coarse,
    side,
    edges,
    ext,
    pairs,
    win1,
    win2,
    count1,
    count2,
    mix,
    spread,
    peaks,
    c_send,
    c_recv,
    p_send,
    p_recv,
    w1_send,
    w1_recv,
    w2_send,
    w2_recv,
):
    rows, cols = cs_ref.shape
    tiles, width = off_ref.shape
    slots = ps_ref.shape[1]
    band = lax.axis_index("band")
    tile = lax.axis_index("tile")
    f32 = jnp.float32
    keep = rows

    barrier = pltpu.get_barrier_semaphore()
    has_band = {-1: band > 0, 0: True, 1: band < n_band - 1}

    odd = lax.rem(band, 2) == 1
    paired = {
        -1: jnp.logical_and(has_band[-1], odd),
        1: jnp.logical_and(has_band[1], jnp.logical_not(odd)),
    }
    apart = {
        -1: jnp.logical_and(has_band[-1], jnp.logical_not(odd)),
        1: jnp.logical_and(has_band[1], odd),
    }

    def when(cond, body):
        if cond is True:
            body()
        else:
            pl.when(cond)(body)

    partners = [
        (db, k) for db in (-1, 0, 1) for k in range(n_tile) if (db, k) != (0, 0)
    ]

    def device(db, k):
        return (band + db, lax.rem(tile + k, n_tile))

    for db, k in partners:

        def greet(db=db, k=k):
            pl.semaphore_signal(barrier, inc=1, device_id=device(db, k), device_id_type=MESH)

        when(has_band[db], greet)

    loads = [
        pltpu.make_async_copy(src, dst, arrived.at[i])
        for i, (src, dst) in enumerate(
            (
                (cs_ref, coarse.at[1, 0]),
                (ct_ref, coarse.at[1, 1]),
                (ps_ref, pairs.at[1, tile, 0]),
                (pt_ref, pairs.at[1, tile, 1]),
                (off_ref, fine.at[0]),
                (tm_ref, fine.at[1]),
                (sm_ref, fine.at[2]),
                (cnt_ref, cells),
            )
        )
    ]
    for load in loads:
        load.start()
    stores = [
        pltpu.make_async_copy(src, dst, stored.at[i])
        for i, (src, dst) in enumerate(
            (
                (u_out, out_ref.at[0:rows]),
                (v_out, out_ref.at[rows : 2 * rows]),
                (sp_out, out_ref.at[2 * rows : 2 * rows + tiles]),
                (tp_out, out_ref.at[2 * rows + tiles : 2 * rows + 2 * tiles]),
            )
        )
    ]
    for db in (-1, 1):

        def blank(db=db):
            coarse[1 + db] = jnp.zeros((2, rows, cols), f32)
            for t in range(n_tile):
                pairs[1 + db, t] = jnp.full((2, 1, slots), -1, jnp.int32)
                win1[1 + db, t] = jnp.zeros((tiles, width), f32)
                win2[1 + db, t] = jnp.zeros((tiles, width), f32)
            for dt in range(2):
                side[1 + db, dt] = jnp.zeros((rows, cols), f32)

        pl.when(jnp.logical_not(has_band[db]))(blank)
    for dt in (-1, 1):
        here = tile + dt

        @pl.when(jnp.logical_or(here < 0, here > n_tile - 1))
        def _(dt=dt):
            for db in (-1, 0, 1):
                side[1 + db, (1 + dt) // 2] = jnp.zeros((rows, cols), f32)

    half = cols // 2
    edge_lane = lax.broadcasted_iota(jnp.int32, (rows, cols), 1)
    loads[0].wait()
    loads[1].wait()
    own_cs = coarse[1, 0]
    turned = pltpu.roll(coarse[1, 1], half, 1)
    edges[1] = jnp.where(edge_lane >= half, own_cs, turned)
    edges[0] = jnp.where(edge_lane < half, own_cs, turned)
    one_side = n_tile
    greeters = n_tile - 1
    greeters = greeters + jnp.where(band > 0, one_side, 0) + jnp.where(
        band < n_band - 1, one_side, 0
    )
    pl.semaphore_wait(barrier, greeters)

    def coarse_refs(db, dt):
        if dt == 0:
            return coarse.at[1], coarse.at[1 + db]
        return edges.at[(1 - dt) // 2], side.at[1 + db, (1 + dt) // 2]

    def coarse_copy(db, dt):
        return pltpu.make_async_remote_copy(
            src_ref=coarse_refs(-db, -dt)[0],
            dst_ref=coarse_refs(-db, -dt)[1],
            send_sem=c_send.at[1 + db, 1 + dt],
            recv_sem=c_recv.at[1 - db, 1 - dt],
            device_id=(band + db, tile + dt),
            device_id_type=MESH,
        )

    def coarse_in(db, dt):
        return pltpu.make_async_remote_copy(
            src_ref=coarse_refs(db, dt)[0],
            dst_ref=coarse_refs(db, dt)[1],
            send_sem=c_send.at[1 - db, 1 - dt],
            recv_sem=c_recv.at[1 + db, 1 + dt],
            device_id=(band + db, tile + dt),
            device_id_type=MESH,
        )

    around = [(db, dt) for dt in (-1, 1, 0) for db in (-1, 0, 1) if (db, dt) != (0, 0)]

    def there(db, dt):
        ok = None
        for d, at, n in ((db, band, n_band), (dt, tile, n_tile)):
            if d:
                c = at > 0 if d < 0 else at < n - 1
                ok = c if ok is None else jnp.logical_and(ok, c)
        return ok

    for db, dt in around:
        when(there(db, dt), lambda db=db, dt=dt: coarse_copy(db, dt).start())

    def pair_copy(db, k):
        return pltpu.make_async_remote_copy(
            src_ref=pairs.at[1, tile],
            dst_ref=pairs.at[1 - db, tile],
            send_sem=p_send.at[1 + db, k],
            recv_sem=p_recv.at[1 - db, tile],
            device_id=device(db, k),
            device_id_type=MESH,
        )

    def pair_in(db, k):
        src = lax.rem(tile + k, n_tile)
        return pltpu.make_async_remote_copy(
            src_ref=pairs.at[1, tile],
            dst_ref=pairs.at[1 + db, src],
            send_sem=p_send.at[1 + db, k],
            recv_sem=p_recv.at[1 + db, src],
            device_id=device(db, k),
            device_id_type=MESH,
        )

    loads[2].wait()
    loads[3].wait()
    for db, k in partners:
        when(has_band[db], lambda db=db, k=k: pair_copy(db, k).start())

    full = n_tile * width
    scale = float(full * full) / 4.0 * entropy
    near_i = lax.broadcasted_iota(jnp.int32, (width, width), 0)
    near_j = lax.broadcasted_iota(jnp.int32, (width, width), 1)
    mix_high, mix_low = halves(jnp.exp((near_i * near_j).astype(f32) * (2.0 / scale)))
    mix[0:width, 0:width] = mix_high
    mix[width : 2 * width, 0:width] = mix_high
    mix[0:width, width : 2 * width] = mix_low
    mix[width : 2 * width, width : 2 * width] = jnp.zeros((width, width), jnp.bfloat16)
    cell = lax.broadcasted_iota(jnp.int32, (1, width), 1)
    lift, ease = [], []
    for t in range(n_tile):
        gap = (t - tile) * width
        lift.append((-cell * cell - 2 * gap * cell).astype(f32) * (1.0 / scale))
        rest = (gap - cell).astype(f32)
        ease.append(jnp.exp(rest * rest * (-1.0 / scale)))

    base = (band - 1) * n_tile * tiles
    window = 3 * n_tile * tiles

    def hits(count, index):
        return jnp.where(
            lax.broadcasted_iota(jnp.int32, (count, slots), 0) == index, 1.0, 0.0
        ).astype(jnp.bfloat16)

    total = lax.dot_general(
        hits(tiles, pairs[1, tile, 0]),
        hits(window, pairs[1, tile, 1] - base),
        NT,
        preferred_element_type=f32,
    )
    lane = lax.broadcasted_iota(jnp.int32, (tiles, window), 1)
    own = lax.broadcasted_iota(jnp.int32, (tiles, window), 0)
    drow = (
        own + tiles - (lane // (n_tile * tiles)) * tiles - lane % tiles
    ).astype(f32)
    damp = drow * drow * (-1.0 / scale)
    count1[...] = total

    for db, dt in around:
        when(there(db, dt), lambda db=db, dt=dt: coarse_in(db, dt).wait_recv())

    span_r = rows + 2 * keep
    wide = 2 * cols
    grid_rows = n_band * rows
    for which in range(2):
        for db in (-1, 0, 1):
            lo = which * rows
            if db == -1:
                rs, rd = slice(lo + rows - keep, lo + rows), slice(0, keep)
            elif db == 0:
                rs, rd = slice(lo, lo + rows), slice(keep, keep + rows)
            else:
                rs, rd = slice(lo, lo + keep), slice(keep + rows, span_r)
            rs = slice(rs.start - lo, rs.stop - lo)
            ext[which, rd, 0:cols] = coarse[1 + db, which, rs]
            left, right = side[1 + db, 0, rs], side[1 + db, 1, rs]
            if which == 0:
                both = jnp.where(edge_lane < half, right, left)
            else:
                both = pltpu.roll(jnp.where(edge_lane < half, left, right), half, 1)
            ext[which, rd, cols:wide] = both
    src_ext = ext[0]
    tgt_ext = ext[1]
    row_at = lax.broadcasted_iota(jnp.int32, (span_r, wide), 0) + band * rows - keep
    lane_at = lax.broadcasted_iota(jnp.int32, (span_r, wide), 1)
    col_at = jnp.where(lane_at < cols + cols // 2, lane_at, lane_at - wide) + tile * cols
    inside = jnp.logical_and(
        jnp.logical_and(row_at >= 0, row_at < grid_rows),
        jnp.logical_and(col_at >= 0, col_at < n_tile * cols),
    )

    def blur(field, lost):
        n = field.shape[0] - 2 * REACH
        across = taps[0] * field[0:n]
        for k in range(1, 2 * REACH + 1):
            across = across + taps[k] * field[k : k + n]
        result = taps[REACH] * across
        for k in range(1, REACH + 1):
            result = result + taps[REACH + k] * (
                pltpu.roll(across, k, 1) + pltpu.roll(across, wide - k, 1)
            )
        return result

    def power(x):
        return jnp.exp(coarse_power * jnp.log(x))

    def ones_blur(position, count):
        out = jnp.zeros(position.shape, f32)
        for k in range(-REACH, REACH + 1):
            at = position + k
            out = out + jnp.where(jnp.logical_and(at >= 0, at < count), taps[REACH + k], 0.0)
        return out

    edge_r = ones_blur(row_at[:, 0:1], grid_rows)
    edge_c = ones_blur(col_at[0:1, :], n_tile * cols)
    safe = jnp.where(inside, edge_r * edge_c, 1.0)
    safe_src = jnp.where(inside, src_ext, 1.0)
    safe_tgt = jnp.where(inside, tgt_ext, 1.0)
    u = jnp.where(inside, power(safe_src / safe), 0.0)
    for lost in (4, 8, 12):
        field = u if lost == 4 else (v if lost == 8 else u)
        out = blur(field, lost)
        s = slice(lost, span_r - lost)
        mask = inside[s]
        mass = safe_src[s] if lost == 8 else safe_tgt[s]
        res = jnp.where(mask, power(mass / jnp.where(mask, out, 1.0)), 0.0)
        if lost == 8:
            u = res
        else:
            v = res
    u_out[...] = u[keep - 8 : keep - 8 + rows, 0:cols]
    scaling_v = v[keep - 12 : keep - 12 + rows, 0:cols]
    v_out[...] = scaling_v
    stores[0].start()
    stores[1].start()

    fold = tiles // rows
    log_v = jnp.log(scaling_v)
    parent = jnp.broadcast_to(log_v[:, None, :], (rows, fold, cols)).reshape(tiles, cols)
    for load in loads[4:]:
        load.wait()
    field = (fine[0] + entropy * parent) / entropy + jnp.log(fine[1])

    def gather(win, send, recv, value, between, absorb):
        win[1, tile] = value

        def outward(db, k):
            return pltpu.make_async_remote_copy(
                src_ref=win.at[1, tile],
                dst_ref=win.at[1 - db, tile],
                send_sem=send.at[1 + db, k],
                recv_sem=recv.at[1 - db, tile],
                device_id=device(db, k),
                device_id_type=MESH,
            )

        def onward(db, k):
            src = lax.rem(tile + k, n_tile)
            return pltpu.make_async_remote_copy(
                src_ref=win.at[1, src],
                dst_ref=win.at[1 - db, src],
                send_sem=send.at[1 + db, k],
                recv_sem=recv.at[1 - db, src],
                device_id=device(db, 0),
                device_id_type=MESH,
            )

        def arrive(db, k):
            src = lax.rem(tile + k, n_tile)
            return pltpu.make_async_remote_copy(
                src_ref=win.at[1, tile],
                dst_ref=win.at[1 + db, src],
                send_sem=send.at[1 + db, k],
                recv_sem=recv.at[1 + db, src],
                device_id=device(db, k),
                device_id_type=MESH,
            )

        order = sorted(range(1, n_tile), key=lambda k: min(k, n_tile - k))
        for k in order:
            outward(0, k).start()
        for k in [0] + order:
            for db in (-1, 1):
                go = apart[db] if k else has_band[db]
                when(go, lambda db=db, k=k: outward(db, k).start())
        for k in order:
            arrive(0, k).wait_recv()
            for db in (-1, 1):
                when(paired[db], lambda db=db, k=k: onward(db, k).start())
        between()
        absorb(1)
        for db in (-1, 1):

            def take(db=db):
                for k in [0] + order:
                    arrive(db, k).wait_recv()

            when(has_band[db], take)
            absorb(1 + db)

        def finish():
            for db, k in partners:
                go = apart[db] if db and k else has_band[db]
                when(go, lambda db=db, k=k: outward(db, k).wait_send())
                if db and k:
                    when(paired[db], lambda db=db, k=k: onward(db, k).wait_send())

        return finish

    per_band = n_tile * tiles

    def absorber(win):
        def absorb(b):
            lifted = jnp.concatenate([win[b, t] + lift[t] for t in range(n_tile)], axis=0)
            high = jnp.max(lifted, axis=1, keepdims=True)
            near = jnp.concatenate(halves(jnp.exp(lifted - high)), axis=1)
            out = lax.dot_general(near, mix[...], NN, preferred_element_type=f32)
            out = out[:, 0:width] + out[:, width : 2 * width]
            for t in range(n_tile):
                part = out[t * tiles : (t + 1) * tiles] * ease[t]
                part_high, part_low = halves(part)
                rows_at = slice(b * per_band + t * tiles, b * per_band + (t + 1) * tiles)
                spread[rows_at, 0:width] = part_high
                spread[rows_at, width : 2 * width] = part_low
            peaks[:, b * per_band : (b + 1) * per_band] = column_to_row(high, per_band)

        return absorb

    def reduce(count):
        n = count[...]
        lifted = jnp.where(n > 0.0, peaks[...] + damp, -jnp.inf)
        peak = jnp.max(lifted, axis=1, keepdims=True)
        weight = n * jnp.exp(lifted - peak)
        both = jnp.concatenate(halves(weight), axis=0)
        out = lax.dot_general(both, spread[...], NN, preferred_element_type=f32)
        summed = out[0:tiles, 0:width] + (
            out[tiles : 2 * tiles, 0:width] + out[0:tiles, width : 2 * width]
        )
        return peak + jnp.log(summed)

    mine = (band * n_tile + tile) * tiles

    def counts_of(b, t):
        at = (b * n_tile + t) * tiles
        count2[:, at : at + tiles] = lax.dot_general(
            hits(tiles, pairs[b, t, 1] - mine),
            hits(tiles, pairs[b, t, 0]),
            NT,
            preferred_element_type=f32,
        )

    blocks = [(b, t) for b in range(3) for t in range(n_tile)]

    def early_counts():
        for db, k in partners:
            when(has_band[db], lambda db=db, k=k: pair_in(db, k).wait_recv())
        for b, t in blocks[0 : len(blocks) // 2]:
            counts_of(b, t)

    def late_counts():
        for b, t in blocks[len(blocks) // 2 :]:
            counts_of(b, t)

    finish1 = gather(win1, w1_send, w1_recv, field, early_counts, absorber(win1))
    potential = -damping * entropy * reduce(count1)
    sp_out[...] = potential
    eye = lax.broadcasted_iota(jnp.int32, (tiles, tiles), 0) == lax.broadcasted_iota(
        jnp.int32, (tiles, tiles), 1
    )
    cell_count = jnp.sum(jnp.where(eye, cells[...].astype(f32), 0.0), axis=1, keepdims=True)
    active = lax.broadcasted_iota(jnp.int32, (tiles, width), 1).astype(f32) < cell_count
    source_field = jnp.where(active, potential / entropy + jnp.log(fine[2]), -jnp.inf)
    finish2 = gather(
        win2, w2_send, w2_recv, source_field, late_counts, absorber(win2)
    )
    stores[2].start()
    tp_out[...] = -damping * entropy * reduce(count2)
    stores[3].start()

    for db, dt in around:
        when(there(db, dt), lambda db=db, dt=dt: coarse_copy(db, dt).wait_send())
    for db, k in partners:
        when(has_band[db], lambda db=db, k=k: pair_copy(db, k).wait_send())
    finish1()
    finish2()
    for store in stores:
        store.wait()


def write_out(packed, *outs):
    at = 0
    for out in outs:
        count = out.shape[0]
        out[...] = packed[at : at + count]
        at += count


def per_device(cs, ct, off, sm, tm, cnt, ps, pt):
    n_band = lax.axis_size("band")
    n_tile = lax.axis_size("tile")
    rows, cols = cs.shape
    tiles, width = off.shape
    f32 = jnp.float32
    slots = ps.shape[0]
    window = 3 * n_tile * tiles
    dma = pltpu.SemaphoreType.DMA
    shapes = (
        jax.ShapeDtypeStruct((rows, cols), f32),
        jax.ShapeDtypeStruct((rows, cols), f32),
        jax.ShapeDtypeStruct((tiles, width), f32),
        jax.ShapeDtypeStruct((tiles, width), f32),
    )
    packed = pl.pallas_call(
        functools.partial(kernel, n_band, n_tile),
        out_shape=jax.ShapeDtypeStruct((2 * rows + 2 * tiles, width), f32),
        in_specs=[pl.BlockSpec(memory_space=pltpu.HBM)] * 8,
        out_specs=pl.BlockSpec(memory_space=pltpu.HBM),
        scratch_shapes=[
            pltpu.VMEM((3, tiles, width), f32),
            pltpu.VMEM((1, tiles), jnp.int32),
            dma((8,)),
            pltpu.VMEM((rows, cols), f32),
            pltpu.VMEM((rows, cols), f32),
            pltpu.VMEM((tiles, width), f32),
            pltpu.VMEM((tiles, width), f32),
            dma((4,)),
            pltpu.VMEM((3, 2, rows, cols), f32),
            pltpu.VMEM((3, 2, rows, cols), f32),
            pltpu.VMEM((2, rows, cols), f32),
            pltpu.VMEM((2, 3 * rows, 2 * cols), f32),
            pltpu.VMEM((3, n_tile, 2, 1, slots), jnp.int32),
            pltpu.VMEM((3, n_tile, tiles, width), f32),
            pltpu.VMEM((3, n_tile, tiles, width), f32),
            pltpu.VMEM((tiles, window), f32),
            pltpu.VMEM((tiles, window), f32),
            pltpu.VMEM((2 * width, 2 * width), jnp.bfloat16),
            pltpu.VMEM((window, 2 * width), jnp.bfloat16),
            pltpu.VMEM((1, window), f32),
            dma((3, 3)),
            dma((3, 3)),
            dma((3, n_tile)),
            dma((3, n_tile)),
            dma((3, n_tile)),
            dma((3, n_tile)),
            dma((3, n_tile)),
            dma((3, n_tile)),
        ],
        compiler_params=pltpu.CompilerParams(
            collective_id=0, has_side_effects=True, vmem_limit_bytes=60 * 1024 * 1024
        ),
    )(cs, ct, off, sm, tm, cnt.reshape(1, tiles), ps.reshape(1, slots), pt.reshape(1, slots))
    return pl.pallas_call(
        write_out,
        out_shape=shapes,
        compiler_params=pltpu.CompilerParams(vmem_limit_bytes=60 * 1024 * 1024),
    )(packed)


def solution(mesh):
    placed = (
        P("band", "tile"),
        P("band", "tile"),
        P(("band", "tile"), None),
        P(("band", "tile"), None),
        P(("band", "tile"), None),
        P(("band", "tile")),
        P(("band", "tile")),
        P(("band", "tile")),
    )
    return jax.shard_map(
        per_device,
        mesh=mesh,
        in_specs=placed,
        out_specs=(
            P("band", "tile"),
            P("band", "tile"),
            P(("band", "tile"), None),
            P(("band", "tile"), None),
        ),
        check_vma=False,
    )
```

```python
import functools
import math

import jax
import jax.numpy as jnp
from jax import lax
from jax.experimental import pallas as pl
from jax.experimental.pallas import tpu as pltpu
from jax.sharding import PartitionSpec as P

COARSE_ITERS = 2
REACH = 4
entropy = 0.5
damping = 0.8
coarse_power = 0.8
taps = [math.exp(-0.125 * k * k) for k in range(-REACH, REACH + 1)]
MESH = pl.DeviceIdType.MESH
NT = (((1,), (1,)), ((), ()))
NN = (((1,), (0,)), ((), ()))


def halves(x):
    high = x.astype(jnp.bfloat16)
    low = (x - high.astype(jnp.float32)).astype(jnp.bfloat16)
    return high, low


def column_to_row(col, tiles):
    out = []
    for at in range(0, tiles, 128):
        eye = lax.broadcasted_iota(jnp.int32, (128, 128), 0) == lax.broadcasted_iota(
            jnp.int32, (128, 128), 1
        )
        part = jnp.where(eye, col[at : at + 128], 0.0)
        out.append(jnp.sum(part, axis=0, keepdims=True))
    return jnp.concatenate(out, axis=1)


def kernel(
    n_band,
    n_tile,
    cs_ref,
    ct_ref,
    off_ref,
    sm_ref,
    tm_ref,
    cnt_ref,
    ps_ref,
    pt_ref,
    out_ref,
    fine,
    cells,
    arrived,
    u_out,
    v_out,
    sp_out,
    tp_out,
    stored,
    coarse,
    side,
    edges,
    ext,
    pairs,
    win1,
    win2,
    count1,
    count2,
    mix,
    spread,
    peaks,
    c_send,
    c_recv,
    p_send,
    p_recv,
    w1_send,
    w1_recv,
    w2_send,
    w2_recv,
):
    rows, cols = cs_ref.shape
    tiles, width = off_ref.shape
    slots = ps_ref.shape[1]
    band = lax.axis_index("band")
    tile = lax.axis_index("tile")
    f32 = jnp.float32
    keep = rows

    barrier = pltpu.get_barrier_semaphore()
    has_band = {-1: band > 0, 0: True, 1: band < n_band - 1}

    odd = lax.rem(band, 2) == 1
    paired = {
        -1: jnp.logical_and(has_band[-1], odd),
        1: jnp.logical_and(has_band[1], jnp.logical_not(odd)),
    }
    apart = {
        -1: jnp.logical_and(has_band[-1], jnp.logical_not(odd)),
        1: jnp.logical_and(has_band[1], odd),
    }

    def when(cond, body):
        if cond is True:
            body()
        else:
            pl.when(cond)(body)

    partners = [
        (db, k) for db in (-1, 0, 1) for k in range(n_tile) if (db, k) != (0, 0)
    ]

    def device(db, k):
        return (band + db, lax.rem(tile + k, n_tile))

    for db, k in partners:

        def greet(db=db, k=k):
            pl.semaphore_signal(barrier, inc=1, device_id=device(db, k), device_id_type=MESH)

        when(has_band[db], greet)

    loads = [
        pltpu.make_async_copy(src, dst, arrived.at[i])
        for i, (src, dst) in enumerate(
            (
                (cs_ref, coarse.at[1, 0]),
                (ct_ref, coarse.at[1, 1]),
                (ps_ref, pairs.at[1, tile, 0]),
                (pt_ref, pairs.at[1, tile, 1]),
                (off_ref, fine.at[0]),
                (tm_ref, fine.at[1]),
                (sm_ref, fine.at[2]),
                (cnt_ref, cells),
            )
        )
    ]
    for load in loads:
        load.start()
    stores = [
        pltpu.make_async_copy(src, dst, stored.at[i])
        for i, (src, dst) in enumerate(
            (
                (u_out, out_ref.at[0:rows]),
                (v_out, out_ref.at[rows : 2 * rows]),
                (sp_out, out_ref.at[2 * rows : 2 * rows + tiles]),
                (tp_out, out_ref.at[2 * rows + tiles : 2 * rows + 2 * tiles]),
            )
        )
    ]
    for db in (-1, 1):

        def blank(db=db):
            coarse[1 + db] = jnp.zeros((2, rows, cols), f32)
            for t in range(n_tile):
                pairs[1 + db, t] = jnp.full((2, 1, slots), -1, jnp.int32)
                win1[1 + db, t] = jnp.zeros((tiles, width), f32)
                win2[1 + db, t] = jnp.zeros((tiles, width), f32)
            for dt in range(2):
                side[1 + db, dt] = jnp.zeros((rows, cols), f32)

        pl.when(jnp.logical_not(has_band[db]))(blank)
    for dt in (-1, 1):
        here = tile + dt

        @pl.when(jnp.logical_or(here < 0, here > n_tile - 1))
        def _(dt=dt):
            for db in (-1, 0, 1):
                side[1 + db, (1 + dt) // 2] = jnp.zeros((rows, cols), f32)

    half = cols // 2
    edge_lane = lax.broadcasted_iota(jnp.int32, (rows, cols), 1)
    loads[0].wait()
    loads[1].wait()
    own_cs = coarse[1, 0]
    turned = pltpu.roll(coarse[1, 1], half, 1)
    edges[1] = jnp.where(edge_lane >= half, own_cs, turned)
    edges[0] = jnp.where(edge_lane < half, own_cs, turned)
    one_side = n_tile
    greeters = n_tile - 1
    greeters = greeters + jnp.where(band > 0, one_side, 0) + jnp.where(
        band < n_band - 1, one_side, 0
    )
    pl.semaphore_wait(barrier, greeters)

    def coarse_refs(db, dt):
        if dt == 0:
            return coarse.at[1], coarse.at[1 + db]
        return edges.at[(1 - dt) // 2], side.at[1 + db, (1 + dt) // 2]

    def coarse_copy(db, dt):
        return pltpu.make_async_remote_copy(
            src_ref=coarse_refs(-db, -dt)[0],
            dst_ref=coarse_refs(-db, -dt)[1],
            send_sem=c_send.at[1 + db, 1 + dt],
            recv_sem=c_recv.at[1 - db, 1 - dt],
            device_id=(band + db, tile + dt),
            device_id_type=MESH,
        )

    def coarse_in(db, dt):
        return pltpu.make_async_remote_copy(
            src_ref=coarse_refs(db, dt)[0],
            dst_ref=coarse_refs(db, dt)[1],
            send_sem=c_send.at[1 - db, 1 - dt],
            recv_sem=c_recv.at[1 + db, 1 + dt],
            device_id=(band + db, tile + dt),
            device_id_type=MESH,
        )

    around = [(db, dt) for dt in (0, -1, 1) for db in (0, -1, 1) if (db, dt) != (0, 0)]

    def there(db, dt):
        ok = None
        for d, at, n in ((db, band, n_band), (dt, tile, n_tile)):
            if d:
                c = at > 0 if d < 0 else at < n - 1
                ok = c if ok is None else jnp.logical_and(ok, c)
        return ok

    for db, dt in around:
        when(there(db, dt), lambda db=db, dt=dt: coarse_copy(db, dt).start())

    def pair_copy(db, k):
        return pltpu.make_async_remote_copy(
            src_ref=pairs.at[1, tile],
            dst_ref=pairs.at[1 - db, tile],
            send_sem=p_send.at[1 + db, k],
            recv_sem=p_recv.at[1 - db, tile],
            device_id=device(db, k),
            device_id_type=MESH,
        )

    def pair_in(db, k):
        src = lax.rem(tile + k, n_tile)
        return pltpu.make_async_remote_copy(
            src_ref=pairs.at[1, tile],
            dst_ref=pairs.at[1 + db, src],
            send_sem=p_send.at[1 + db, k],
            recv_sem=p_recv.at[1 + db, src],
            device_id=device(db, k),
            device_id_type=MESH,
        )

    loads[2].wait()
    loads[3].wait()
    for db, k in partners:
        when(has_band[db], lambda db=db, k=k: pair_copy(db, k).start())

    full = n_tile * width
    scale = float(full * full) / 4.0 * entropy
    near_i = lax.broadcasted_iota(jnp.int32, (width, width), 0)
    near_j = lax.broadcasted_iota(jnp.int32, (width, width), 1)
    mix_high, mix_low = halves(jnp.exp((near_i * near_j).astype(f32) * (2.0 / scale)))
    mix[0:width, 0:width] = mix_high
    mix[width : 2 * width, 0:width] = mix_high
    mix[0:width, width : 2 * width] = mix_low
    mix[width : 2 * width, width : 2 * width] = jnp.zeros((width, width), jnp.bfloat16)
    cell = lax.broadcasted_iota(jnp.int32, (1, width), 1)
    lift, ease = [], []
    for t in range(n_tile):
        gap = (t - tile) * width
        lift.append((-cell * cell - 2 * gap * cell).astype(f32) * (1.0 / scale))
        rest = (gap - cell).astype(f32)
        ease.append(jnp.exp(rest * rest * (-1.0 / scale)))

    base = (band - 1) * n_tile * tiles
    window = 3 * n_tile * tiles

    def hits(count, index):
        return jnp.where(
            lax.broadcasted_iota(jnp.int32, (count, slots), 0) == index, 1.0, 0.0
        ).astype(jnp.bfloat16)

    total = lax.dot_general(
        hits(tiles, pairs[1, tile, 0]),
        hits(window, pairs[1, tile, 1] - base),
        NT,
        preferred_element_type=f32,
    )
    lane = lax.broadcasted_iota(jnp.int32, (tiles, window), 1)
    own = lax.broadcasted_iota(jnp.int32, (tiles, window), 0)
    drow = (
        own + tiles - (lane // (n_tile * tiles)) * tiles - lane % tiles
    ).astype(f32)
    damp = drow * drow * (-1.0 / scale)
    count1[...] = total

    for db, dt in around:
        when(there(db, dt), lambda db=db, dt=dt: coarse_in(db, dt).wait_recv())

    span_r = rows + 2 * keep
    wide = 2 * cols
    grid_rows = n_band * rows
    for which in range(2):
        for db in (-1, 0, 1):
            lo = which * rows
            if db == -1:
                rs, rd = slice(lo + rows - keep, lo + rows), slice(0, keep)
            elif db == 0:
                rs, rd = slice(lo, lo + rows), slice(keep, keep + rows)
            else:
                rs, rd = slice(lo, lo + keep), slice(keep + rows, span_r)
            rs = slice(rs.start - lo, rs.stop - lo)
            ext[which, rd, 0:cols] = coarse[1 + db, which, rs]
            left, right = side[1 + db, 0, rs], side[1 + db, 1, rs]
            if which == 0:
                both = jnp.where(edge_lane < half, right, left)
            else:
                both = pltpu.roll(jnp.where(edge_lane < half, left, right), half, 1)
            ext[which, rd, cols:wide] = both
    src_ext = ext[0]
    tgt_ext = ext[1]
    row_at = lax.broadcasted_iota(jnp.int32, (span_r, wide), 0) + band * rows - keep
    lane_at = lax.broadcasted_iota(jnp.int32, (span_r, wide), 1)
    col_at = jnp.where(lane_at < cols + cols // 2, lane_at, lane_at - wide) + tile * cols
    inside = jnp.logical_and(
        jnp.logical_and(row_at >= 0, row_at < grid_rows),
        jnp.logical_and(col_at >= 0, col_at < n_tile * cols),
    )

    def blur(field, lost):
        n = field.shape[0] - 2 * REACH
        across = taps[0] * field[0:n]
        for k in range(1, 2 * REACH + 1):
            across = across + taps[k] * field[k : k + n]
        result = taps[REACH] * across
        for k in range(1, REACH + 1):
            result = result + taps[REACH + k] * (
                pltpu.roll(across, k, 1) + pltpu.roll(across, wide - k, 1)
            )
        return result

    def power(x):
        return jnp.exp(coarse_power * jnp.log(x))

    def ones_blur(position, count):
        out = jnp.zeros(position.shape, f32)
        for k in range(-REACH, REACH + 1):
            at = position + k
            out = out + jnp.where(jnp.logical_and(at >= 0, at < count), taps[REACH + k], 0.0)
        return out

    edge_r = ones_blur(row_at[:, 0:1], grid_rows)
    edge_c = ones_blur(col_at[0:1, :], n_tile * cols)
    safe = jnp.where(inside, edge_r * edge_c, 1.0)
    safe_src = jnp.where(inside, src_ext, 1.0)
    safe_tgt = jnp.where(inside, tgt_ext, 1.0)
    u = jnp.where(inside, power(safe_src / safe), 0.0)
    for lost in (4, 8, 12):
        field = u if lost == 4 else (v if lost == 8 else u)
        out = blur(field, lost)
        s = slice(lost, span_r - lost)
        mask = inside[s]
        mass = safe_src[s] if lost == 8 else safe_tgt[s]
        res = jnp.where(mask, power(mass / jnp.where(mask, out, 1.0)), 0.0)
        if lost == 8:
            u = res
        else:
            v = res
    u_out[...] = u[keep - 8 : keep - 8 + rows, 0:cols]
    scaling_v = v[keep - 12 : keep - 12 + rows, 0:cols]
    v_out[...] = scaling_v
    stores[0].start()
    stores[1].start()

    fold = tiles // rows
    log_v = jnp.log(scaling_v)
    parent = jnp.broadcast_to(log_v[:, None, :], (rows, fold, cols)).reshape(tiles, cols)
    for load in loads[4:]:
        load.wait()
    field = (fine[0] + entropy * parent) / entropy + jnp.log(fine[1])

    def gather(win, send, recv, value, between, absorb):
        win[1, tile] = value

        def outward(db, k):
            return pltpu.make_async_remote_copy(
                src_ref=win.at[1, tile],
                dst_ref=win.at[1 - db, tile],
                send_sem=send.at[1 + db, k],
                recv_sem=recv.at[1 - db, tile],
                device_id=device(db, k),
                device_id_type=MESH,
            )

        def onward(db, k):
            src = lax.rem(tile + k, n_tile)
            return pltpu.make_async_remote_copy(
                src_ref=win.at[1, src],
                dst_ref=win.at[1 - db, src],
                send_sem=send.at[1 + db, k],
                recv_sem=recv.at[1 - db, src],
                device_id=device(db, 0),
                device_id_type=MESH,
            )

        def arrive(db, k):
            src = lax.rem(tile + k, n_tile)
            return pltpu.make_async_remote_copy(
                src_ref=win.at[1, tile],
                dst_ref=win.at[1 + db, src],
                send_sem=send.at[1 + db, k],
                recv_sem=recv.at[1 + db, src],
                device_id=device(db, k),
                device_id_type=MESH,
            )

        order = sorted(range(1, n_tile), key=lambda k: min(k, n_tile - k))
        for k in order:
            outward(0, k).start()
        for k in [0] + order:
            for db in (-1, 1):
                go = apart[db] if k else has_band[db]
                when(go, lambda db=db, k=k: outward(db, k).start())
        for k in order:
            arrive(0, k).wait_recv()
            for db in (-1, 1):
                when(paired[db], lambda db=db, k=k: onward(db, k).start())
        between()
        absorb(1)
        for db in (-1, 1):

            def take(db=db):
                for k in [0] + order:
                    arrive(db, k).wait_recv()

            when(has_band[db], take)
            absorb(1 + db)

        def finish():
            for db, k in partners:
                go = apart[db] if db and k else has_band[db]
                when(go, lambda db=db, k=k: outward(db, k).wait_send())
                if db and k:
                    when(paired[db], lambda db=db, k=k: onward(db, k).wait_send())

        return finish

    per_band = n_tile * tiles

    def absorber(win):
        def absorb(b):
            lifted = jnp.concatenate([win[b, t] + lift[t] for t in range(n_tile)], axis=0)
            high = jnp.max(lifted, axis=1, keepdims=True)
            near = jnp.concatenate(halves(jnp.exp(lifted - high)), axis=1)
            out = lax.dot_general(near, mix[...], NN, preferred_element_type=f32)
            out = out[:, 0:width] + out[:, width : 2 * width]
            for t in range(n_tile):
                part = out[t * tiles : (t + 1) * tiles] * ease[t]
                part_high, part_low = halves(part)
                rows_at = slice(b * per_band + t * tiles, b * per_band + (t + 1) * tiles)
                spread[rows_at, 0:width] = part_high
                spread[rows_at, width : 2 * width] = part_low
            peaks[:, b * per_band : (b + 1) * per_band] = column_to_row(high, per_band)

        return absorb

    def reduce(count):
        n = count[...]
        lifted = jnp.where(n > 0.0, peaks[...] + damp, -jnp.inf)
        peak = jnp.max(lifted, axis=1, keepdims=True)
        weight = n * jnp.exp(lifted - peak)
        both = jnp.concatenate(halves(weight), axis=0)
        out = lax.dot_general(both, spread[...], NN, preferred_element_type=f32)
        summed = out[0:tiles, 0:width] + (
            out[tiles : 2 * tiles, 0:width] + out[0:tiles, width : 2 * width]
        )
        return peak + jnp.log(summed)

    mine = (band * n_tile + tile) * tiles

    def counts_of(b, t):
        at = (b * n_tile + t) * tiles
        count2[:, at : at + tiles] = lax.dot_general(
            hits(tiles, pairs[b, t, 1] - mine),
            hits(tiles, pairs[b, t, 0]),
            NT,
            preferred_element_type=f32,
        )

    blocks = [(b, t) for b in range(3) for t in range(n_tile)]

    def early_counts():
        for db, k in partners:
            when(has_band[db], lambda db=db, k=k: pair_in(db, k).wait_recv())
        for b, t in blocks[0 : len(blocks) // 2]:
            counts_of(b, t)

    def late_counts():
        for b, t in blocks[len(blocks) // 2 :]:
            counts_of(b, t)

    finish1 = gather(win1, w1_send, w1_recv, field, early_counts, absorber(win1))
    potential = -damping * entropy * reduce(count1)
    sp_out[...] = potential
    eye = lax.broadcasted_iota(jnp.int32, (tiles, tiles), 0) == lax.broadcasted_iota(
        jnp.int32, (tiles, tiles), 1
    )
    cell_count = jnp.sum(jnp.where(eye, cells[...].astype(f32), 0.0), axis=1, keepdims=True)
    active = lax.broadcasted_iota(jnp.int32, (tiles, width), 1).astype(f32) < cell_count
    source_field = jnp.where(active, potential / entropy + jnp.log(fine[2]), -jnp.inf)
    finish2 = gather(
        win2, w2_send, w2_recv, source_field, late_counts, absorber(win2)
    )
    stores[2].start()
    tp_out[...] = -damping * entropy * reduce(count2)
    stores[3].start()

    for db, dt in around:
        when(there(db, dt), lambda db=db, dt=dt: coarse_copy(db, dt).wait_send())
    for db, k in partners:
        when(has_band[db], lambda db=db, k=k: pair_copy(db, k).wait_send())
    finish1()
    finish2()
    for store in stores:
        store.wait()


def write_out(packed, *outs):
    at = 0
    for out in outs:
        count = out.shape[0]
        out[...] = packed[at : at + count]
        at += count


def per_device(cs, ct, off, sm, tm, cnt, ps, pt):
    n_band = lax.axis_size("band")
    n_tile = lax.axis_size("tile")
    rows, cols = cs.shape
    tiles, width = off.shape
    f32 = jnp.float32
    slots = ps.shape[0]
    window = 3 * n_tile * tiles
    dma = pltpu.SemaphoreType.DMA
    shapes = (
        jax.ShapeDtypeStruct((rows, cols), f32),
        jax.ShapeDtypeStruct((rows, cols), f32),
        jax.ShapeDtypeStruct((tiles, width), f32),
        jax.ShapeDtypeStruct((tiles, width), f32),
    )
    packed = pl.pallas_call(
        functools.partial(kernel, n_band, n_tile),
        out_shape=jax.ShapeDtypeStruct((2 * rows + 2 * tiles, width), f32),
        in_specs=[pl.BlockSpec(memory_space=pltpu.HBM)] * 8,
        out_specs=pl.BlockSpec(memory_space=pltpu.HBM),
        scratch_shapes=[
            pltpu.VMEM((3, tiles, width), f32),
            pltpu.VMEM((1, tiles), jnp.int32),
            dma((8,)),
            pltpu.VMEM((rows, cols), f32),
            pltpu.VMEM((rows, cols), f32),
            pltpu.VMEM((tiles, width), f32),
            pltpu.VMEM((tiles, width), f32),
            dma((4,)),
            pltpu.VMEM((3, 2, rows, cols), f32),
            pltpu.VMEM((3, 2, rows, cols), f32),
            pltpu.VMEM((2, rows, cols), f32),
            pltpu.VMEM((2, 3 * rows, 2 * cols), f32),
            pltpu.VMEM((3, n_tile, 2, 1, slots), jnp.int32),
            pltpu.VMEM((3, n_tile, tiles, width), f32),
            pltpu.VMEM((3, n_tile, tiles, width), f32),
            pltpu.VMEM((tiles, window), f32),
            pltpu.VMEM((tiles, window), f32),
            pltpu.VMEM((2 * width, 2 * width), jnp.bfloat16),
            pltpu.VMEM((window, 2 * width), jnp.bfloat16),
            pltpu.VMEM((1, window), f32),
            dma((3, 3)),
            dma((3, 3)),
            dma((3, n_tile)),
            dma((3, n_tile)),
            dma((3, n_tile)),
            dma((3, n_tile)),
            dma((3, n_tile)),
            dma((3, n_tile)),
        ],
        compiler_params=pltpu.CompilerParams(
            collective_id=0, has_side_effects=True, vmem_limit_bytes=60 * 1024 * 1024
        ),
    )(cs, ct, off, sm, tm, cnt.reshape(1, tiles), ps.reshape(1, slots), pt.reshape(1, slots))
    return pl.pallas_call(
        write_out,
        out_shape=shapes,
        compiler_params=pltpu.CompilerParams(vmem_limit_bytes=60 * 1024 * 1024),
    )(packed)


def solution(mesh):
    placed = (
        P("band", "tile"),
        P("band", "tile"),
        P(("band", "tile"), None),
        P(("band", "tile"), None),
        P(("band", "tile"), None),
        P(("band", "tile")),
        P(("band", "tile")),
        P(("band", "tile")),
    )
    return jax.shard_map(
        per_device,
        mesh=mesh,
        in_specs=placed,
        out_specs=(
            P("band", "tile"),
            P("band", "tile"),
            P(("band", "tile"), None),
            P(("band", "tile"), None),
        ),
        check_vma=False,
    )
```
